128 devices in a mesh: gx: 8 (over x, core), gy: 16 (over y, z).
Axes of the slice: x: 4, y: 4, z: 4, core: 2. Of those that a mesh axis runs over, the one named last changes fastest.
Arguments:
- adjoint_state: float32 [192, 256, 4096], P(None, 'gx', 'gy'), may hold values from -6 to 6
- inverse_scale: float32 [256, 4096], P('gx', 'gy'), may hold values from 0.35 to 1.2
- element_inverse: float32 [192, 192], replicated, may hold values from -0.4375 to 0.4375
- trace_op: float32 [96, 192], replicated, may hold values from -0.4375 to 0.4375
- lift_op: float32 [192, 96], replicated, may hold values from -0.625 to 0.625
- obs_elem: int32 [2, 98304], P(None, ('gx', 'gy')), may hold values from 0 to 1048575, as said below
- obs_count: int32 [2, 128], P(None, ('gx', 'gy')), may hold values from 6 to 768, as said below
- obs_basis: float32 [2, 64, 98304], P(None, None, ('gx', 'gy')), may hold values from -5 to 5
- innovation: float32 [2, 98304], P(None, ('gx', 'gy')), may hold values from -5 to 5
Outputs:
- adjoint_out: float32 [192, 256, 4096], P(None, 'gx', 'gy')
The draws below stay inside these ranges and needn't reach their ends.
Inputs may be any that keep to these rules, and one draw needn't show every extreme that they name: `obs_elem`: among the live observations of one device in one step, at most 6 lie in elements of any one device; in every step the first 6 slots of each device are live and all lie in elements of one device. `obs_count`: device 0 has all 768 slots live in every step.
All inputs are finite; a program needn't handle non-finite values.
Results may differ from the reference program's by a relative error of at most 0.0001.
Values sent between devices are 32-bit elements; how exact they have to be, the bound alone decides.
A program may use at most 128 MiB of HBM per device.

```python
import math
import jax
import jax.numpy as jnp
from jax import lax

NODES = 64
FN = 24
STATE = 192
EX = 32
EY = 256
STEPS = 2
OBS_DEV = 768
NEX = 256
NEY = 4096
TOTAL_OBS = 98304
N_GX = 8
N_GY = 16


def draw_obs_elem(key, part):
    key = jax.random.fold_in(key, 11)
    devices_all = N_GX * N_GY
    capacity = OBS_DEV // devices_all
    first_key, second_key = jax.random.split(key)
    scores = jax.random.randint(first_key, (STEPS, devices_all, devices_all), 0, 1 << 20) * devices_all + jnp.arange(devices_all, dtype=jnp.int32)
    order = jnp.argsort(scores, axis=-1).astype(jnp.int32)
    segment = jnp.arange(OBS_DEV, dtype=jnp.int32) // capacity
    target = order[:, :, segment]
    local_elem = jax.random.randint(second_key, (STEPS, devices_all, OBS_DEV), 0, EX * EY)
    row_index = target // N_GY * EX + local_elem // EY
    column_index = target % N_GY * EY + local_elem % EY
    return (row_index * (EY * N_GY) + column_index).reshape(STEPS, devices_all * OBS_DEV).astype(jnp.int32)


def draw_obs_count(key, part):
    key = jax.random.fold_in(key, 23)
    devices_all = N_GX * N_GY
    counts = jax.random.randint(key, (STEPS, devices_all), OBS_DEV // devices_all, OBS_DEV + 1)
    return counts.at[:, 0].set(OBS_DEV).astype(jnp.int32)


def levels(own_key, dims, cuts, smallest, high):
    level = 1.0
    for dim, blocks in cuts:
        draws = jax.random.uniform(jax.random.fold_in(jax.random.fold_in(own_key, 6), dim), (blocks,), jnp.float32, smallest / len(cuts), high / len(cuts))
        level = level * jnp.repeat(jnp.exp(draws), dims[dim] // blocks).reshape((-1,) + (1,) * (len(dims) - 1 - dim))
    return level


def centred(stream_key, extent, scale, reach, cuts=(), kind=jnp.bfloat16):
    values = scale * jax.random.normal(stream_key, extent, jnp.float32)
    if cuts:
        values = values * levels(stream_key, extent, cuts, -0.22, 0.18)
    return jnp.clip(values, -reach, reach).astype(kind)


def setup_inputs(seed: int = 0) -> dict:
    streams_of = jax.random.split(jax.random.key(seed), 10)
    return {
        "adjoint_state": centred(streams_of[0], (STATE, NEX, NEY), 1.0, 6.0, ((1, 8), (2, 16)), jnp.float32),
        "inverse_scale": jnp.clip(jnp.exp(math.log(1.2) - 1.23214374 * jax.random.uniform(streams_of[1], (NEX, NEY), jnp.float32) ** levels(streams_of[1], (NEX, NEY), ((0, 8), (1, 16)), -0.2, 0.2)), 0.35, 1.2),
        "element_inverse": centred(streams_of[2], (STATE, STATE), STATE ** -0.5, 0.4375, (), jnp.float32),
        "trace_op": centred(streams_of[3], (4 * FN, STATE), STATE ** -0.5, 0.4375, (), jnp.float32),
        "lift_op": centred(streams_of[4], (STATE, 4 * FN), (4 * FN) ** -0.5, 0.625, (), jnp.float32),
        "obs_elem": draw_obs_elem(jax.random.fold_in(streams_of[9], 71), 0),
        "obs_count": draw_obs_count(jax.random.fold_in(streams_of[9], 71), 0),
        "obs_basis": centred(streams_of[7], (STEPS, NODES, TOTAL_OBS), 1.0, 5.0, ((2, 128),), jnp.float32),
        "innovation": centred(streams_of[8], (STEPS, TOTAL_OBS), 1.0, 5.0, ((1, 128),), jnp.float32),
    }


def condensed(state, inverse_scale, element_inverse, trace_op, lift_op):
    rows = state.shape[0]
    flat = state.reshape(rows, -1)
    traces = jnp.dot(trace_op, flat, precision=lax.Precision.HIGHEST).reshape(4, FN, NEX, NEY)
    west_face, east_face, south_face, north_face = traces[0], traces[1], traces[2], traces[3]
    from_west = jnp.roll(east_face, 1, axis=1)
    from_east = jnp.roll(west_face, -1, axis=1)
    from_south = jnp.concatenate([south_face[:, :, :1], north_face[:, :, :-1]], axis=2)
    from_north = jnp.concatenate([south_face[:, :, 1:], north_face[:, :, -1:]], axis=2)
    numerical = 0.5 * (traces + jnp.stack([from_west, from_east, from_south, from_north]))
    lifted = flat + jnp.dot(lift_op, numerical.reshape(4 * FN, -1), precision=lax.Precision.HIGHEST)
    updated = jnp.dot(element_inverse, lifted, precision=lax.Precision.HIGHEST)
    return updated.reshape(rows, NEX, NEY) * inverse_scale[None, :, :]


def reference(adjoint_state, inverse_scale, element_inverse, trace_op, lift_op, obs_elem, obs_count, obs_basis, innovation):
    state = adjoint_state
    slots = jnp.arange(TOTAL_OBS, dtype=jnp.int32)
    for which_step in range(STEPS):
        owner_count = obs_count[which_step][slots // OBS_DEV]
        live = (slots % OBS_DEV) < owner_count
        payload = jnp.where(live[None, :], obs_basis[which_step] * innovation[which_step][None, :], jnp.zeros_like(obs_basis[which_step]))
        target = jnp.where(live, obs_elem[which_step], jnp.zeros_like(obs_elem[which_step])).astype(jnp.int32)
        forcing = jnp.zeros((NODES, NEX * NEY), jnp.float32).at[:, target].add(payload)
        state = state.at[:NODES].add(forcing.reshape(NODES, NEX, NEY))
        state = condensed(state, inverse_scale, element_inverse, trace_op, lift_op)
    return state
```

```python
import functools

import jax
import jax.numpy as jnp
from jax import lax
from jax.experimental import pallas as pl
from jax.experimental.pallas import tpu as pltpu
from jax.sharding import PartitionSpec as P

F32 = jnp.float32
BF = jnp.bfloat16
MESH = pl.DeviceIdType.MESH
STEPS = 2
NODES = 64
FN = 24
STATE = 192
EX = 32
EY = 256
OBS = 768
CAP = 6
GX = 8
GY = 16
DEV = GX * GY
VMEM = pl.BlockSpec(memory_space=pltpu.VMEM)
SMEM = pl.BlockSpec(memory_space=pltpu.SMEM)
ANY = pl.BlockSpec(memory_space=pl.ANY)


def dot(a, b):
    return jnp.dot(a, b, preferred_element_type=F32)


def dot_nt(a, b):
    return lax.dot_general(a, b, (((1,), (1,)), ((), ())), preferred_element_type=F32)


def dot_full(a, b):
    return jnp.dot(a, b, preferred_element_type=F32, precision=lax.Precision.HIGHEST)


def split(v):
    hi = v.astype(BF)
    return hi, (v - hi.astype(F32)).astype(BF)


def iota(shape, dim):
    return lax.broadcasted_iota(jnp.int32, shape, dim)


def pack(elem_ref, count_ref, basis_ref, innov_ref, out_ref):
    lane = iota((1, OBS), 1)
    owner = iota((DEV, OBS), 0)
    tri = (iota((256, 256), 0) < iota((256, 256), 1)).astype(F32).astype(BF)
    row = iota((128, OBS), 0)
    halves = []
    ids = jnp.zeros((DEV, 128), F32)
    for s in range(STEPS):
        elem = elem_ref[s : s + 1, :]
        gx = lax.shift_right_logical(elem, 17)
        lx = lax.shift_right_logical(elem, 12) & (EX - 1)
        gy = lax.shift_right_logical(elem, 8) & (GY - 1)
        ly = elem & (EY - 1)
        live = lane < count_ref[s, 0]
        target = jnp.where(live, gx * GY + gy, -1)
        member = (owner == target).astype(F32)
        carry = jnp.zeros((DEV, 1), F32)
        running = []
        for b in range(OBS // 256):
            part = member[:, b * 256 : (b + 1) * 256]
            running.append(dot(part.astype(BF), tri) + carry)
            carry = carry + jnp.sum(part, axis=1, keepdims=True)
        before = jnp.concatenate(running, axis=1)
        rank = jnp.sum(member * before, axis=0, keepdims=True).astype(jnp.int32)
        hi, lo = split(basis_ref[s] * innov_ref[s : s + 1, :])
        both = jnp.concatenate([hi, lo], axis=0)
        picked = []
        for j in range(CAP):
            chosen = jnp.where(rank == j, member, 0.0).astype(BF)
            got = dot_nt(chosen, both)
            picked.append(got + pltpu.roll(got, 64, 1))
        halves.append(picked)
        where = jnp.where(row == rank + 16 * s, lx + 1, 0)
        where = where + jnp.where(row == rank + 16 * s + 8, ly, 0)
        ids = ids + dot_nt(member.astype(BF), where.astype(F32).astype(BF))
    low = iota((DEV, 128), 1) < 64
    for j in range(CAP):
        out_ref[pl.ds(j, DEV, stride=8), :] = jnp.where(low, halves[0][j], halves[1][j])
    out_ref[pl.ds(CAP, DEV, stride=8), :] = ids
    out_ref[pl.ds(CAP + 1, DEV, stride=8), :] = jnp.zeros((DEV, 128), F32)


def route_kernel(elem_ref, count_ref, basis_ref, innov_ref, got_ref, out_ref, send_sem, recv_sem):
    px, py = lax.axis_index("gx"), lax.axis_index("gy")
    me = px * GY + py
    barrier = pltpu.get_barrier_semaphore()

    def greet(k, carry):
        peer = (me + k) % DEV
        pl.semaphore_signal(
            barrier, inc=1, device_id=(peer // GY, peer % GY), device_id_type=MESH
        )
        return carry

    lax.fori_loop(1, DEV, greet, 0)
    pack(elem_ref, count_ref, basis_ref, innov_ref, out_ref)
    pl.semaphore_wait(barrier, DEV - 1)
    mine = pl.ds(pl.multiple_of(me * 8, 8), 8)

    def send(k, carry):
        peer = (me + k) % DEV
        pltpu.make_async_remote_copy(
            src_ref=out_ref.at[pl.ds(pl.multiple_of(peer * 8, 8), 8)],
            dst_ref=got_ref.at[mine],
            send_sem=send_sem,
            recv_sem=recv_sem,
            device_id=(peer // GY, peer % GY),
            device_id_type=MESH,
        ).start()
        return carry

    lax.fori_loop(1, DEV, send, 0)
    got_ref[mine, :] = out_ref[mine, :]
    rest = pl.ds(0, (DEV - 1) * 8)
    pltpu.make_async_copy(out_ref.at[rest], out_ref.at[rest], send_sem).wait()
    pltpu.make_async_copy(got_ref.at[rest], got_ref.at[rest], recv_sem).wait()


def route(obs_elem, obs_count, obs_basis, innovation):
    return pl.pallas_call(
        route_kernel,
        out_shape=pltpu.VMEM((DEV * 8, 128), F32),
        in_specs=[VMEM, SMEM, VMEM, VMEM],
        out_specs=VMEM,
        scratch_shapes=[
            pltpu.VMEM((DEV * 8, 128), F32),
            pltpu.SemaphoreType.DMA,
            pltpu.SemaphoreType.DMA,
        ],
        compiler_params=pltpu.CompilerParams(
            collective_id=0, has_side_effects=True, vmem_limit_bytes=24 << 20
        ),
        name="route",
    )(obs_elem, obs_count, obs_basis, innovation)


def unpack(got_ref, pay_ref, col_ref, rowid_ref):
    ids = got_ref[pl.ds(CAP, DEV, stride=8), :].T
    parts = [got_ref[pl.ds(j, DEV, stride=8), :].T for j in range(CAP)]
    for s in range(STEPS):
        values = jnp.concatenate([p[s * 64 : s * 64 + 64] for p in parts], axis=1)
        hi, lo = split(values)
        pay_ref[s, 0:64, :] = hi
        pay_ref[s, 64:128, :] = lo
        xs = [ids[s * 16 + j : s * 16 + j + 1, :] for j in range(CAP)]
        ys = [ids[s * 16 + 8 + j : s * 16 + 9 + j, :] for j in range(CAP)]
        rowid_ref[s : s + 1, :] = jnp.concatenate(xs, axis=1).astype(jnp.int32) - 1
        ycol = jnp.concatenate(ys, axis=1).astype(jnp.int32)
        hot = (iota((EY, OBS), 0) == ycol).astype(F32)
        col_ref[s] = hot.T.astype(BF)


def force(s, pay_ref, col_ref, rowid_ref, force_ref):
    group = 4

    def body(g, carry):
        rowid = rowid_ref[s : s + 1, :]
        pay = pay_ref[s]
        stack = []
        for i in range(group):
            here = (rowid == g * group + i).astype(F32).astype(BF)
            stack.append(pay * here)
        got = dot(jnp.concatenate(stack, axis=0), col_ref[s])
        for i in range(group):
            top = got[i * 128 : i * 128 + 64]
            force_ref[s, g * group + i] = top + got[i * 128 + 64 : i * 128 + 128]
        return carry

    lax.fori_loop(0, EX // group, body, 0)


def order(i):
    return jnp.where(i == 0, 0, jnp.where(i == 1, EX - 1, i - 1))


def traces(x, state, t_ref, near_ref, carry):
    down, up = carry
    hi, lo = state
    tr = dot(t_ref[0], hi) + dot(t_ref[1], hi) + dot(t_ref[0], lo)
    west, east = tr[0:FN], tr[FN : 2 * FN]
    south, north = tr[2 * FN : 3 * FN], tr[3 * FN : 4 * FN]
    near_ref[x, FN : 2 * FN, :] = west
    near_ref[x + 2, 0:FN, :] = east
    from_south = pltpu.roll(north, 1, 1)
    from_north = pltpu.roll(south, EY - 1, 1)
    near_ref[x + 1, 2 * FN : 3 * FN, :] = from_south
    near_ref[x + 1, 3 * FN : 4 * FN, :] = from_north
    here = iota((FN, 128), 1) == x
    up = jnp.where(here, from_south[:, 0:1], up)
    down = jnp.where(here, from_north[:, EY - 1 : EY], down)
    return down, up


def patch(near_ref, below, above):
    first = iota((FN, 128), 1) == 0
    last = iota((FN, 128), 1) == 127

    def body(x, carry):
        low = pltpu.roll(below, (128 - x) % 128, 1)
        high = pltpu.roll(above, 127 - x, 1)
        s_rows, n_rows = slice(2 * FN, 3 * FN), slice(3 * FN, 4 * FN)
        near_ref[x + 1, s_rows, 0:128] = jnp.where(first, low, near_ref[x + 1, s_rows, 0:128])
        near_ref[x + 1, n_rows, 128:256] = jnp.where(
            last, high, near_ref[x + 1, n_rows, 128:256]
        )
        return carry

    lax.fori_loop(0, EX, body, 0, unroll=2)


def finish(x, acc_ref, near_ref, b_ref, scale_ref):
    hi, lo = split(near_ref[x + 1])
    lifted = dot(b_ref[0], hi) + dot(b_ref[1], hi) + dot(b_ref[0], lo)
    return (acc_ref[x] + lifted) * scale_ref[pl.ds(x, 1), :]


def steps_kernel(
    state_ref, scale_ref, inverse_ref, trace_ref, lift_ref, got_ref,
    acc_ref, near2_ref, b_ref,
    stage, slab, near1_ref, force_ref, pay_ref, col_ref, rowid_ref, a_ref, t_ref,
    ysend, yrecv, load_sem, send_sem, recv_sem,
):
    px, py = lax.axis_index("gx"), lax.axis_index("gy")
    peers = (
        (lax.rem(px + GX - 1, GX), py),
        (lax.rem(px + 1, GX), py),
        (px, lax.rem(py + GY - 1, GY)),
        (px, lax.rem(py + 1, GY)),
    )
    loads = []
    for c in range(EX // 8):
        for h in range(2):
            loads.append(
                pltpu.make_async_copy(
                    state_ref.at[:, c * 8 : c * 8 + 8, h * 128 : h * 128 + 128],
                    stage.at[c, h],
                    load_sem.at[c, h],
                )
            )
            loads[-1].start()
    barrier = pltpu.get_barrier_semaphore()
    for peer in peers:
        pl.semaphore_signal(barrier, inc=1, device_id=peer, device_id_type=MESH)

    operator = trace_ref[...]
    inverse = inverse_ref[...]
    half = 0.5 * dot_full(inverse, lift_ref[...])
    whole = inverse + dot_full(half, operator)
    for ref, value in ((a_ref, whole), (b_ref, half), (t_ref, operator)):
        hi, lo = split(value)
        ref[0] = hi
        ref[1] = lo
    unpack(got_ref, pay_ref, col_ref, rowid_ref)
    for s in range(STEPS):
        force(s, pay_ref, col_ref, rowid_ref, force_ref)
    for copy in loads:
        copy.wait()
    pl.semaphore_wait(barrier, 4)

    def send_halos(s, near_ref, down, up):
        ysend[s, 0] = down
        ysend[s, 1] = up
        pairs = (
            (near_ref.at[0, FN : 2 * FN], near_ref.at[EX, FN : 2 * FN]),
            (near_ref.at[EX + 1, 0:FN], near_ref.at[1, 0:FN]),
            (ysend.at[s, 0], yrecv.at[s, 1]),
            (ysend.at[s, 1], yrecv.at[s, 0]),
        )
        copies = []
        for k in range(4):
            copies.append(
                pltpu.make_async_remote_copy(
                    src_ref=pairs[k][0],
                    dst_ref=pairs[k][1],
                    send_sem=send_sem.at[s, k],
                    recv_sem=recv_sem.at[s, k],
                    device_id=peers[k],
                    device_id_type=MESH,
                )
            )
            copies[-1].start()
        return copies

    def take_halos(s, near_ref, copies):
        for copy in copies:
            copy.wait()
        below = jnp.where(py == 0, ysend[s, 0], yrecv[s, 0])
        above = jnp.where(py == GY - 1, ysend[s, 1], yrecv[s, 1])
        patch(near_ref, below, above)

    def keep(x, s, value, near_ref, carry):
        value = jnp.concatenate([value[0:NODES] + force_ref[s, x], value[NODES:STATE]], axis=0)
        hi, lo = split(value)
        slab[x, 0] = hi
        slab[x, 1] = lo
        return traces(x, (hi, lo), t_ref, near_ref, carry)

    def first(i, carry):
        x = order(i)
        c, r = x // 8, x % 8
        halves = [stage[c, h, :, pl.ds(r, 1), :].reshape(STATE, 128) for h in range(2)]
        return keep(x, 0, jnp.concatenate(halves, axis=1), near1_ref, carry)

    def middle(i, carry):
        x = order(i)
        return keep(x, 1, finish(x, acc_ref, near1_ref, b_ref, scale_ref), near2_ref, carry)

    def hold(x, carry):
        hi, lo = slab[x, 0], slab[x, 1]
        acc_ref[x] = dot(a_ref[0], hi) + dot(a_ref[1], hi) + dot(a_ref[0], lo)
        return carry

    rim = jnp.zeros((FN, 128), F32)
    down, up = lax.fori_loop(0, EX, first, (rim, rim), unroll=2)
    copies = send_halos(0, near1_ref, down, up)
    lax.fori_loop(0, EX, hold, 0, unroll=2)
    take_halos(0, near1_ref, copies)
    down, up = lax.fori_loop(0, EX, middle, (rim, rim), unroll=2)
    copies = send_halos(1, near2_ref, down, up)
    lax.fori_loop(0, EX, hold, 0, unroll=2)
    take_halos(1, near2_ref, copies)


def steps(state, scale, inverse, trace, lift, got):
    return pl.pallas_call(
        steps_kernel,
        out_shape=(
            pltpu.VMEM((EX, STATE, EY), F32),
            pltpu.VMEM((EX + 2, 4 * FN, EY), F32),
            pltpu.VMEM((2, STATE, 4 * FN), BF),
        ),
        in_specs=[ANY, VMEM, VMEM, VMEM, VMEM, VMEM],
        out_specs=(VMEM, VMEM, VMEM),
        scratch_shapes=[
            pltpu.VMEM((EX // 8, 2, STATE, 8, 128), F32),
            pltpu.VMEM((EX, 2, STATE, EY), BF),
            pltpu.VMEM((EX + 2, 4 * FN, EY), F32),
            pltpu.VMEM((STEPS, EX, NODES, EY), F32),
            pltpu.VMEM((STEPS, 128, OBS), BF),
            pltpu.VMEM((STEPS, OBS, EY), BF),
            pltpu.VMEM((8, OBS), jnp.int32),
            pltpu.VMEM((2, STATE, STATE), BF),
            pltpu.VMEM((2, 4 * FN, STATE), BF),
            pltpu.VMEM((STEPS, 2, FN, 128), F32),
            pltpu.VMEM((STEPS, 2, FN, 128), F32),
            pltpu.SemaphoreType.DMA((EX // 8, 2)),
            pltpu.SemaphoreType.DMA((STEPS, 4)),
            pltpu.SemaphoreType.DMA((STEPS, 4)),
        ],
        compiler_params=pltpu.CompilerParams(
            collective_id=1, has_side_effects=True, vmem_limit_bytes=40 << 20
        ),
        name="steps",
    )(state, scale, inverse, trace, lift, got)


def last_kernel(acc_ref, near_ref, b_ref, scale_ref, out_ref, stage, sem):
    copies = []
    for c in range(EX // 8):

        def body(r, carry):
            x = c * 8 + r
            value = finish(x, acc_ref, near_ref, b_ref, scale_ref)
            for h in range(2):
                stage[c, h, :, pl.ds(r, 1), :] = value[:, h * 128 : h * 128 + 128].reshape(
                    STATE, 1, 128
                )
            return carry

        lax.fori_loop(0, 8, body, 0, unroll=2)
        for h in range(2):
            copies.append(
                pltpu.make_async_copy(
                    stage.at[c, h],
                    out_ref.at[:, c * 8 : c * 8 + 8, h * 128 : h * 128 + 128],
                    sem.at[c, h],
                )
            )
            copies[-1].start()
    for copy in copies:
        copy.wait()


def last(acc, near, lift, scale):
    return pl.pallas_call(
        last_kernel,
        out_shape=jax.ShapeDtypeStruct((STATE, EX, EY), F32),
        in_specs=[VMEM, VMEM, VMEM, VMEM],
        out_specs=ANY,
        scratch_shapes=[
            pltpu.VMEM((EX // 8, 2, STATE, 8, 128), F32),
            pltpu.SemaphoreType.DMA((EX // 8, 2)),
        ],
        compiler_params=pltpu.CompilerParams(vmem_limit_bytes=24 << 20),
        name="last",
    )(acc, near, lift, scale)


def local(
    adjoint_state, inverse_scale, element_inverse, trace_op, lift_op,
    obs_elem, obs_count, obs_basis, innovation,
):
    got = route(obs_elem, obs_count, obs_basis, innovation)
    acc, near, lift = steps(
        adjoint_state, inverse_scale, element_inverse, trace_op, lift_op, got
    )
    return last(acc, near, lift, inverse_scale)


def solution(mesh):
    placed = (
        P(None, "gx", "gy"),
        P("gx", "gy"),
        P(),
        P(),
        P(),
        P(None, ("gx", "gy")),
        P(None, ("gx", "gy")),
        P(None, None, ("gx", "gy")),
        P(None, ("gx", "gy")),
    )
    return jax.shard_map(
        local, mesh=mesh, in_specs=placed, out_specs=P(None, "gx", "gy"), check_vma=False
    )
```

```python
import functools

import jax
import jax.numpy as jnp
from jax import lax
from jax.experimental import pallas as pl
from jax.experimental.pallas import tpu as pltpu
from jax.sharding import PartitionSpec as P

F32 = jnp.float32
BF = jnp.bfloat16
MESH = pl.DeviceIdType.MESH
STEPS = 2
NODES = 64
FN = 24
STATE = 192
EX = 32
EY = 256
OBS = 768
CAP = 6
GX = 8
GY = 16
DEV = GX * GY
VMEM = pl.BlockSpec(memory_space=pltpu.VMEM)
HBM = pl.BlockSpec(memory_space=pltpu.HBM)


def dot(a, b):
    return jnp.dot(a, b, preferred_element_type=F32)


def rows(*parts):
    return jnp.concatenate(parts, axis=0)


def lanes(*parts):
    return jnp.concatenate(parts, axis=1)


def dot_nt(a, b):
    return lax.dot_general(a, b, (((1,), (1,)), ((), ())), preferred_element_type=F32)


def dot_full(a, b):
    return jnp.dot(a, b, preferred_element_type=F32, precision=lax.Precision.HIGHEST)


def split(v):
    hi = v.astype(BF)
    return hi, (v - hi.astype(F32)).astype(BF)


def triple(v):
    hi, lo = split(v)
    return rows(hi, lo, hi)


def weights(v):
    hi, lo = split(v)
    hi, lo = hi.astype(F32), lo.astype(F32)
    return lanes(hi, hi, lo).astype(BF)


def tile(c, h):
    return pl.ds(pl.multiple_of((c * 2 + h) * STATE, 8), STATE)


def row(c, h, r):
    return pl.ds(pl.multiple_of((c * 2 + h) * STATE * 8, 8) + r, STATE, stride=8)


def iota(shape, dim):
    return lax.broadcasted_iota(jnp.int32, shape, dim)


def pack(elem_ref, count_ref, basis_ref, innov_ref, out_ref):
    lane = iota((1, OBS), 1)
    owner = iota((DEV, OBS), 0)
    tri = (iota((256, 256), 0) < iota((256, 256), 1)).astype(F32).astype(BF)
    row = iota((128, OBS), 0)
    halves = []
    ids = jnp.zeros((DEV, 128), F32)
    for s in range(STEPS):
        elem = elem_ref[s : s + 1, :]
        gx = lax.shift_right_logical(elem, 17)
        lx = lax.shift_right_logical(elem, 12) & (EX - 1)
        gy = lax.shift_right_logical(elem, 8) & (GY - 1)
        ly = elem & (EY - 1)
        live = lane < count_ref[0:1, s : s + 1]
        target = jnp.where(live, gx * GY + gy, -1)
        member = (owner == target).astype(F32)
        carry = jnp.zeros((DEV, 1), F32)
        running = []
        for b in range(OBS // 256):
            part = member[:, b * 256 : (b + 1) * 256]
            running.append(dot(part.astype(BF), tri) + carry)
            carry = carry + jnp.sum(part, axis=1, keepdims=True)
        before = jnp.concatenate(running, axis=1)
        rank = jnp.sum(member * before, axis=0, keepdims=True).astype(jnp.int32)
        hi, lo = split(basis_ref[s] * innov_ref[s : s + 1, :])
        both = jnp.concatenate([hi, lo], axis=0)
        picked = []
        for j in range(CAP):
            chosen = jnp.where(rank == j, member, 0.0).astype(BF)
            got = dot_nt(chosen, both)
            picked.append(got + pltpu.roll(got, 64, 1))
        halves.append(picked)
        where = jnp.where(row == rank + 16 * s, lx + 1, 0)
        where = where + jnp.where(row == rank + 16 * s + 8, ly, 0)
        ids = ids + dot_nt(member.astype(BF), where.astype(F32).astype(BF))
    low = iota((DEV, 128), 1) < 64
    for j in range(CAP):
        out_ref[pl.ds(j, DEV, stride=8), :] = jnp.where(low, halves[0][j], halves[1][j])
    out_ref[pl.ds(CAP, DEV, stride=8), :] = ids
    out_ref[pl.ds(CAP + 1, DEV, stride=8), :] = jnp.zeros((DEV, 128), F32)


def unpack(got_ref, pay_ref, col_ref, rowid_ref):
    ids = got_ref[pl.ds(CAP, DEV, stride=8), :].T
    parts = [got_ref[pl.ds(j, DEV, stride=8), :].T for j in range(CAP)]
    for s in range(STEPS):
        values = jnp.concatenate([p[s * 64 : s * 64 + 64] for p in parts], axis=1)
        hi, lo = split(values)
        pay_ref[s, :, 0:OBS] = hi
        pay_ref[s, :, OBS : 2 * OBS] = lo
        xs = [ids[s * 16 + j : s * 16 + j + 1, :] for j in range(CAP)]
        ys = [ids[s * 16 + 8 + j : s * 16 + 9 + j, :] for j in range(CAP)]
        rowid_ref[s : s + 1, :] = jnp.concatenate(xs, axis=1).astype(jnp.int32) - 1
        ycol = jnp.concatenate(ys, axis=1).astype(jnp.int32)
        hot = (iota((EY, OBS), 0) == ycol).astype(F32)
        hot = hot.T.astype(BF)
        col_ref[s, 0:OBS, :] = hot
        col_ref[s, OBS : 2 * OBS, :] = hot


def force(s, pay_ref, col_ref, rowid_ref, force_ref):
    group = 16

    def body(g, carry):
        rowid = rowid_ref[s : s + 1, :]
        pay = pay_ref[s]
        stack = []
        for i in range(group):
            here = (rowid == g * group + i).astype(F32).astype(BF)
            stack.append(pay * lanes(here, here))
        got = dot(rows(*stack), col_ref[s])
        for i in range(group):
            force_ref[s, g * group + i] = got[i * NODES : i * NODES + NODES]
        return carry

    lax.fori_loop(0, EX // group, body, 0)


def put(x, tr, near_ref, carry):
    down, up = carry
    near_ref[x, FN : 2 * FN, :] = tr[0:FN]
    near_ref[x + 2, 0:FN, :] = tr[FN : 2 * FN]
    from_south = pltpu.roll(tr[3 * FN : 4 * FN], 1, 1)
    from_north = pltpu.roll(tr[2 * FN : 3 * FN], EY - 1, 1)
    near_ref[x + 1, 2 * FN : 3 * FN, :] = from_south
    near_ref[x + 1, 3 * FN : 4 * FN, :] = from_north
    here = iota((FN, 128), 1) == x
    up = jnp.where(here, from_south[:, 0:1], up)
    down = jnp.where(here, from_north[:, EY - 1 : EY], down)
    return down, up


def patch(near_ref, below, above):
    first = iota((FN, 128), 1) == 0
    last = iota((FN, 128), 1) == 127
    south, north = slice(2 * FN, 3 * FN), slice(3 * FN, 4 * FN)

    def body(x, carry):
        low = pltpu.roll(below, (128 - x) % 128, 1)
        high = pltpu.roll(above, 127 - x, 1)
        near_ref[x + 1, south, 0:128] = jnp.where(first, low, near_ref[x + 1, south, 0:128])
        near_ref[x + 1, north, 128:256] = jnp.where(last, high, near_ref[x + 1, north, 128:256])
        return carry

    lax.fori_loop(0, EX, body, 0, unroll=8)


def finish(x, acc_ref, near_ref, b_ref, scale_ref):
    lifted = dot(b_ref[...], triple(near_ref[x + 1]))
    return (acc_ref[x] + lifted) * scale_ref[pl.ds(x, 1), :]


def main_kernel(
    state_hbm, scale_hbm, inverse_hbm, trace_hbm, lift_hbm, elem_hbm, count_hbm, basis_hbm, innov_hbm,
    acc_ref, near2_ref, b_ref, scale_ref,
    stage, slab, near1_ref, tr_ref, force_ref, pay_ref, col_ref, rowid_ref, at_ref, c_ref,
    inverse_ref, trace_ref, lift_ref, elem_ref, count_ref, basis_ref, innov_ref,
    out_ref, got_ref, ysend, yrecv,
    load_sem, small_sem, far_sem, near_send, near_recv, all_in,
):
    px, py = lax.axis_index("gx"), lax.axis_index("gy")
    me = px * GY + py
    small = []
    for k, (src, dst) in enumerate(
        (
            (elem_hbm, elem_ref), (count_hbm, count_ref), (basis_hbm, basis_ref),
            (innov_hbm, innov_ref), (inverse_hbm, inverse_ref), (trace_hbm, trace_ref),
            (lift_hbm, lift_ref), (scale_hbm, scale_ref),
        )
    ):
        small.append(pltpu.make_async_copy(src, dst, small_sem.at[k]))
        small[-1].start()

    def load(c, h):
        column = slice(h * 128, h * 128 + 128)
        band = pl.ds(pl.multiple_of(c * 8, 8), 8)
        return pltpu.make_async_copy(
            state_hbm.at[:, band, column], stage.at[tile(c, h)], load_sem.at[c, h]
        )

    for c in range(EX // 8):
        for h in range(2):
            load(c, h).start()
    barrier = pltpu.get_barrier_semaphore()

    row_peers = [((px + k) % GX, py) for k in range(1, GX)]
    column_peers = [(px, (py + k) % GY) for k in range(1, GY)]
    for peer in row_peers + column_peers:
        pl.semaphore_signal(barrier, inc=1, device_id=peer, device_id_type=MESH)
    for copy in small:
        copy.wait()
    operator = trace_ref[...]
    inverse = inverse_ref[...]
    half = 0.5 * dot_full(inverse, lift_ref[...])
    whole = inverse + dot_full(half, operator)
    at_ref[...] = weights(rows(whole, operator))
    c_ref[...] = weights(rows(whole, operator)[:, 0:NODES])
    b_ref[...] = weights(half)
    pl.semaphore_wait(barrier, GX + GY - 2)
    for peer in column_peers:
        pl.semaphore_signal(all_in, inc=1, device_id=peer, device_id_type=MESH)
    pack(elem_ref, count_ref, basis_ref, innov_ref, out_ref)
    mine = pl.ds(pl.multiple_of(me * 8, 8), 8)
    got_ref[mine, :] = out_ref[mine, :]
    pl.semaphore_wait(all_in, GY - 1)

    def send(k):
        peer = (me + k) % DEV
        pltpu.make_async_remote_copy(
            src_ref=out_ref.at[pl.ds(pl.multiple_of(peer * 8, 8), 8)],
            dst_ref=got_ref.at[mine],
            send_sem=far_sem.at[0],
            recv_sem=far_sem.at[1],
            device_id=(peer // GY, peer % GY),
            device_id_type=MESH,
        ).start()

    flat = stage.reshape(EX // 4 * STATE * 8, 128)

    def begin(c, carry):
        for h in range(2):
            load(c, h).wait()
        for r in range(8):
            if r % 4 == 0:
                for u in range(4 * 4):
                    k = c * 32 + r * 4 + u + 1
                    if r * 4 + u == 31:
                        pl.when(k < DEV)(functools.partial(send, k))
                    else:
                        send(k)
            x = c * 8 + r
            halves = [flat[row(c, h, r), :] for h in range(2)]
            both = dot(at_ref[...], triple(lanes(*halves)))
            acc_ref[x] = both[0:STATE]
            tr_ref[x] = both[STATE:]
        return carry

    lax.fori_loop(0, EX // 8, begin, 0)
    rest = pl.ds(0, (DEV - 1) * 8)
    pltpu.make_async_copy(out_ref.at[rest], out_ref.at[rest], far_sem.at[0]).wait()
    pltpu.make_async_copy(got_ref.at[rest], got_ref.at[rest], far_sem.at[1]).wait()
    unpack(got_ref, pay_ref, col_ref, rowid_ref)
    force(0, pay_ref, col_ref, rowid_ref, force_ref)

    peers = (
        (lax.rem(px + GX - 1, GX), py),
        (lax.rem(px + 1, GX), py),
        (px, lax.rem(py + GY - 1, GY)),
        (px, lax.rem(py + 1, GY)),
    )

    def send_halos(s, near_ref, down, up):
        ysend[s, 0] = down
        ysend[s, 1] = up
        pairs = (
            (near_ref.at[0, FN : 2 * FN], near_ref.at[EX, FN : 2 * FN]),
            (near_ref.at[EX + 1, 0:FN], near_ref.at[1, 0:FN]),
            (ysend.at[s, 0], yrecv.at[s, 1]),
            (ysend.at[s, 1], yrecv.at[s, 0]),
        )
        copies = []
        for k in range(4):
            copies.append(
                pltpu.make_async_remote_copy(
                    src_ref=pairs[k][0],
                    dst_ref=pairs[k][1],
                    send_sem=near_send.at[s, k],
                    recv_sem=near_recv.at[s, k],
                    device_id=peers[k],
                    device_id_type=MESH,
                )
            )
            copies[-1].start()
        return copies

    def take_halos(s, near_ref, copies):
        for copy in copies:
            copy.wait()
        below = jnp.where(py == 0, ysend[s, 0], yrecv[s, 0])
        above = jnp.where(py == GY - 1, ysend[s, 1], yrecv[s, 1])
        patch(near_ref, below, above)

    def correct(x, carry):
        both = dot(c_ref[...], triple(force_ref[0, x]))
        acc_ref[x] += both[0:STATE]
        return put(x, tr_ref[x] + both[STATE:], near1_ref, carry)

    def middle(x, carry):
        value = finish(x, acc_ref, near1_ref, b_ref, scale_ref)
        hi, lo = split(rows(value[0:NODES] + force_ref[1, x], value[NODES:STATE]))
        slab[x, 0:STATE, :] = hi
        slab[x, STATE : 2 * STATE, :] = lo
        return carry

    def trace(x, carry):
        tr = dot(at_ref[STATE : STATE + 4 * FN, :], rows(slab[x], slab[x, 0:STATE, :]))
        return put(x, tr, near2_ref, carry)

    def hold(x, carry):
        acc_ref[x] = dot(at_ref[0:STATE, :], rows(slab[x], slab[x, 0:STATE, :]))
        return carry

    rim = jnp.zeros((FN, 128), F32)
    down, up = lax.fori_loop(0, EX, correct, (rim, rim), unroll=8)
    copies = send_halos(0, near1_ref, down, up)
    force(1, pay_ref, col_ref, rowid_ref, force_ref)
    take_halos(0, near1_ref, copies)
    lax.fori_loop(0, EX, middle, 0, unroll=8)
    down, up = lax.fori_loop(0, EX, trace, (rim, rim), unroll=8)
    copies = send_halos(1, near2_ref, down, up)
    lax.fori_loop(0, EX, hold, 0, unroll=8)
    take_halos(1, near2_ref, copies)


def last_kernel(acc_ref, near_ref, b_ref, scale_ref, out_ref, stage, sem):
    def store(c, h):
        band = pl.ds(pl.multiple_of(c * 8, 8), 8)
        column = slice(h * 128, h * 128 + 128)
        return pltpu.make_async_copy(
            stage.at[tile(c, h)], out_ref.at[:, band, column], sem.at[c, h]
        )

    flat = stage.reshape(EX // 4 * STATE * 8, 128)

    def body(c, carry):
        for r in range(8):
            value = finish(c * 8 + r, acc_ref, near_ref, b_ref, scale_ref)
            for h in range(2):
                flat[row(c, h, r), :] = value[:, h * 128 : h * 128 + 128]
        for h in range(2):
            store(c, h).start()
        return carry

    lax.fori_loop(0, EX // 8, body, 0)
    for c in range(EX // 8):
        for h in range(2):
            store(c, h).wait()


def local(
    adjoint_state, inverse_scale, element_inverse, trace_op, lift_op,
    obs_elem, obs_count, obs_basis, innovation,
):
    acc, near, lift, scale = pl.pallas_call(
        main_kernel,
        out_shape=(
            pltpu.VMEM((EX, STATE, EY), F32),
            pltpu.VMEM((EX + 2, 4 * FN, EY), F32),
            pltpu.VMEM((STATE, 12 * FN), BF),
            pltpu.VMEM((EX, EY), F32),
        ),
        in_specs=[HBM] * 9,
        out_specs=(VMEM, VMEM, VMEM, VMEM),
        scratch_shapes=[
            pltpu.VMEM((EX // 4 * STATE, 8, 128), F32),
            pltpu.VMEM((EX, 2 * STATE, EY), BF),
            pltpu.VMEM((EX + 2, 4 * FN, EY), F32),
            pltpu.VMEM((EX, 4 * FN, EY), F32),
            pltpu.VMEM((STEPS, EX, NODES, EY), F32),
            pltpu.VMEM((STEPS, NODES, 2 * OBS), BF),
            pltpu.VMEM((STEPS, 2 * OBS, EY), BF),
            pltpu.VMEM((8, OBS), jnp.int32),
            pltpu.VMEM((STATE + 4 * FN, 3 * STATE), BF),
            pltpu.VMEM((STATE + 4 * FN, 3 * NODES), BF),
            pltpu.VMEM((STATE, STATE), F32),
            pltpu.VMEM((4 * FN, STATE), F32),
            pltpu.VMEM((STATE, 4 * FN), F32),
            pltpu.VMEM((STEPS, OBS), jnp.int32),
            pltpu.VMEM((1, STEPS), jnp.int32),
            pltpu.VMEM((STEPS, NODES, OBS), F32),
            pltpu.VMEM((STEPS, OBS), F32),
            pltpu.VMEM((DEV * 8, 128), F32),
            pltpu.VMEM((DEV * 8, 128), F32),
            pltpu.VMEM((STEPS, 2, FN, 128), F32),
            pltpu.VMEM((STEPS, 2, FN, 128), F32),
            pltpu.SemaphoreType.DMA((EX // 8, 2)),
            pltpu.SemaphoreType.DMA((8,)),
            pltpu.SemaphoreType.DMA((2,)),
            pltpu.SemaphoreType.DMA((STEPS, 4)),
            pltpu.SemaphoreType.DMA((STEPS, 4)),
            pltpu.SemaphoreType.REGULAR,
        ],
        compiler_params=pltpu.CompilerParams(
            collective_id=0, has_side_effects=True, vmem_limit_bytes=40 << 20
        ),
        name="main",
    )(
        *(
            pltpu.with_memory_space_constraint(v, pltpu.HBM)
            for v in (
                adjoint_state, inverse_scale, element_inverse, trace_op, lift_op,
                obs_elem, obs_count.T, obs_basis, innovation,
            )
        )
    )
    return pl.pallas_call(
        last_kernel,
        out_shape=jax.ShapeDtypeStruct((STATE, EX, EY), F32),
        in_specs=[VMEM, VMEM, VMEM, VMEM],
        out_specs=HBM,
        scratch_shapes=[
            pltpu.VMEM((EX // 4 * STATE, 8, 128), F32),
            pltpu.SemaphoreType.DMA((EX // 8, 2)),
        ],
        compiler_params=pltpu.CompilerParams(vmem_limit_bytes=24 << 20),
        name="last",
    )(acc, near, lift, scale)


def solution(mesh):
    placed = (
        P(None, "gx", "gy"),
        P("gx", "gy"),
        P(),
        P(),
        P(),
        P(None, ("gx", "gy")),
        P(None, ("gx", "gy")),
        P(None, None, ("gx", "gy")),
        P(None, ("gx", "gy")),
    )
    return jax.shard_map(
        local, mesh=mesh, in_specs=placed, out_specs=P(None, "gx", "gy"), check_vma=False
    )
```

```python
import functools

import jax
import jax.numpy as jnp
from jax import lax
from jax.experimental import pallas as pl
from jax.experimental.pallas import tpu as pltpu
from jax.sharding import PartitionSpec as P

F32 = jnp.float32
BF = jnp.bfloat16
MESH = pl.DeviceIdType.MESH
STEPS = 2
NODES = 64
FN = 24
STATE = 192
EX = 32
EY = 256
OBS = 768
CAP = 6
USED = CAP + 1
GX = 8
GY = 16
DEV = GX * GY
VMEM = pl.BlockSpec(memory_space=pltpu.VMEM)
HBM = pl.BlockSpec(memory_space=pltpu.HBM)


def dot(a, b):
    return jnp.dot(a, b, preferred_element_type=F32)


def rows(*parts):
    return jnp.concatenate(parts, axis=0)


def lanes(*parts):
    return jnp.concatenate(parts, axis=1)


def dot_nt(a, b):
    return lax.dot_general(a, b, (((1,), (1,)), ((), ())), preferred_element_type=F32)


def dot_full(a, b):
    return jnp.dot(a, b, preferred_element_type=F32, precision=lax.Precision.HIGHEST)


def split(v):
    hi = v.astype(BF)
    return hi, (v - hi.astype(F32)).astype(BF)


def triple(v):
    hi, lo = split(v)
    return rows(hi, lo, hi)


def weights(v):
    hi, lo = split(v)
    hi, lo = hi.astype(F32), lo.astype(F32)
    return lanes(hi, hi, lo).astype(BF)


def tile(c, h):
    return pl.ds(pl.multiple_of((c * 2 + h) * STATE, 8), STATE)


def row(c, h, r):
    return pl.ds(pl.multiple_of((c * 2 + h) * STATE * 8, 8) + r, STATE, stride=8)


def iota(shape, dim):
    return lax.broadcasted_iota(jnp.int32, shape, dim)


def pack(elem_ref, count_ref, basis_ref, innov_ref, out_ref):
    lane = iota((1, OBS), 1)
    owner = iota((DEV, OBS), 0)
    tri = (iota((256, 256), 0) < iota((256, 256), 1)).astype(F32).astype(BF)
    row = iota((128, OBS), 0)
    halves = []
    ids = jnp.zeros((DEV, 128), F32)
    for s in range(STEPS):
        elem = elem_ref[s : s + 1, :]
        gx = lax.shift_right_logical(elem, 17)
        lx = lax.shift_right_logical(elem, 12) & (EX - 1)
        gy = lax.shift_right_logical(elem, 8) & (GY - 1)
        ly = elem & (EY - 1)
        live = lane < count_ref[0:1, s : s + 1]
        target = jnp.where(live, gx * GY + gy, -1)
        member = (owner == target).astype(F32)
        carry = jnp.zeros((DEV, 1), F32)
        running = []
        for b in range(OBS // 256):
            part = member[:, b * 256 : (b + 1) * 256]
            running.append(dot(part.astype(BF), tri) + carry)
            carry = carry + jnp.sum(part, axis=1, keepdims=True)
        before = jnp.concatenate(running, axis=1)
        rank = jnp.sum(member * before, axis=0, keepdims=True).astype(jnp.int32)
        hi, lo = split(basis_ref[s] * innov_ref[s : s + 1, :])
        both = jnp.concatenate([hi, lo], axis=0)
        picked = []
        for j in range(CAP):
            chosen = jnp.where(rank == j, member, 0.0).astype(BF)
            got = dot_nt(chosen, both)
            picked.append(got + pltpu.roll(got, 64, 1))
        halves.append(picked)
        where = jnp.where(row == rank + 16 * s, lx + 1, 0)
        where = where + jnp.where(row == rank + 16 * s + 8, ly, 0)
        ids = ids + dot_nt(member.astype(BF), where.astype(F32).astype(BF))
    low = iota((DEV, 128), 1) < 64
    for j in range(CAP):
        out_ref[pl.ds(j, DEV, stride=8), :] = jnp.where(low, halves[0][j], halves[1][j])
    out_ref[pl.ds(CAP, DEV, stride=8), :] = ids


def unpack(got_ref, pay_ref, col_ref, rowid_ref):
    ids = got_ref[pl.ds(CAP, DEV, stride=8), :].T
    parts = [got_ref[pl.ds(j, DEV, stride=8), :].T for j in range(CAP)]
    for s in range(STEPS):
        values = jnp.concatenate([p[s * 64 : s * 64 + 64] for p in parts], axis=1)
        hi, lo = split(values)
        pay_ref[s, :, 0:OBS] = hi
        pay_ref[s, :, OBS : 2 * OBS] = lo
        xs = [ids[s * 16 + j : s * 16 + j + 1, :] for j in range(CAP)]
        ys = [ids[s * 16 + 8 + j : s * 16 + 9 + j, :] for j in range(CAP)]
        rowid_ref[s : s + 1, :] = jnp.concatenate(xs, axis=1).astype(jnp.int32) - 1
        ycol = jnp.concatenate(ys, axis=1).astype(jnp.int32)
        hot = (iota((EY, OBS), 0) == ycol).astype(F32)
        hot = hot.T.astype(BF)
        col_ref[s, 0:OBS, :] = hot
        col_ref[s, OBS : 2 * OBS, :] = hot


def force(s, pay_ref, col_ref, rowid_ref, force_ref):
    group = 16

    def body(g, carry):
        rowid = rowid_ref[s : s + 1, :]
        pay = pay_ref[s]
        stack = []
        for i in range(group):
            here = (rowid == g * group + i).astype(F32).astype(BF)
            stack.append(pay * lanes(here, here))
        got = dot(rows(*stack), col_ref[s])
        for i in range(group):
            force_ref[s, g * group + i] = got[i * NODES : i * NODES + NODES]
        return carry

    lax.fori_loop(0, EX // group, body, 0)


def put(x, tr, near_ref, carry):
    down, up = carry
    near_ref[x, FN : 2 * FN, :] = tr[0:FN]
    near_ref[x + 2, 0:FN, :] = tr[FN : 2 * FN]
    from_south = pltpu.roll(tr[3 * FN : 4 * FN], 1, 1)
    from_north = pltpu.roll(tr[2 * FN : 3 * FN], EY - 1, 1)
    near_ref[x + 1, 2 * FN : 3 * FN, :] = from_south
    near_ref[x + 1, 3 * FN : 4 * FN, :] = from_north
    here = iota((FN, 128), 1) == x
    up = jnp.where(here, from_south[:, 0:1], up)
    down = jnp.where(here, from_north[:, EY - 1 : EY], down)
    return down, up


def patch(near_ref, below, above):
    first = iota((FN, 128), 1) == 0
    last = iota((FN, 128), 1) == 127
    south, north = slice(2 * FN, 3 * FN), slice(3 * FN, 4 * FN)

    def body(x, carry):
        low = pltpu.roll(below, (128 - x) % 128, 1)
        high = pltpu.roll(above, 127 - x, 1)
        near_ref[x + 1, south, 0:128] = jnp.where(first, low, near_ref[x + 1, south, 0:128])
        near_ref[x + 1, north, 128:256] = jnp.where(last, high, near_ref[x + 1, north, 128:256])
        return carry

    lax.fori_loop(0, EX, body, 0, unroll=8)


def finish(x, acc_ref, near_ref, b_ref, scale_ref):
    lifted = dot(b_ref[...], triple(near_ref[x + 1]))
    return (acc_ref[x] + lifted) * scale_ref[pl.ds(x, 1), :]


def main_kernel(
    state_hbm, scale_hbm, inverse_hbm, trace_hbm, lift_hbm, elem_hbm, count_hbm, basis_hbm, innov_hbm,
    acc_ref, near2_ref, b_ref, scale_ref,
    stage, slab, near1_ref, tr_ref, force_ref, pay_ref, col_ref, rowid_ref, at_ref, c_ref,
    inverse_ref, trace_ref, lift_ref, elem_ref, count_ref, basis_ref, innov_ref,
    out_ref, got_ref, ysend, yrecv,
    load_sem, small_sem, far_sem, near_send, near_recv, all_in,
):
    px, py = lax.axis_index("gx"), lax.axis_index("gy")
    me = px * GY + py
    small = []
    for k, (src, dst) in enumerate(
        (
            (elem_hbm, elem_ref), (count_hbm, count_ref), (basis_hbm, basis_ref),
            (innov_hbm, innov_ref), (inverse_hbm, inverse_ref), (trace_hbm, trace_ref),
            (lift_hbm, lift_ref), (scale_hbm, scale_ref),
        )
    ):
        small.append(pltpu.make_async_copy(src, dst, small_sem.at[k]))
        small[-1].start()

    def load(c, h):
        column = slice(h * 128, h * 128 + 128)
        band = pl.ds(pl.multiple_of(c * 8, 8), 8)
        return pltpu.make_async_copy(
            state_hbm.at[:, band, column], stage.at[tile(c, h)], load_sem.at[c, h]
        )

    for c in range(EX // 8):
        for h in range(2):
            load(c, h).start()
    barrier = pltpu.get_barrier_semaphore()

    row_peers = [((px + k) % GX, py) for k in range(1, GX)]
    column_peers = [(px, (py + k) % GY) for k in range(1, GY)]
    for peer in row_peers + column_peers:
        pl.semaphore_signal(barrier, inc=1, device_id=peer, device_id_type=MESH)
    for copy in small[0:4]:
        copy.wait()
    pack(elem_ref, count_ref, basis_ref, innov_ref, out_ref)
    mine = pl.ds(pl.multiple_of(me * 8, 8), USED)
    got_ref[mine, :] = out_ref[mine, :]
    pl.semaphore_wait(barrier, GX + GY - 2)
    for peer in column_peers:
        pl.semaphore_signal(all_in, inc=1, device_id=peer, device_id_type=MESH)

    def send(peer):
        to = peer[0] * GY + peer[1]
        pltpu.make_async_remote_copy(
            src_ref=out_ref.at[pl.ds(pl.multiple_of(to * 8, 8), USED)],
            dst_ref=got_ref.at[mine],
            send_sem=far_sem.at[0],
            recv_sem=far_sem.at[1],
            device_id=peer,
            device_id_type=MESH,
        ).start()

    for peer in row_peers + column_peers:
        send(peer)
    for copy in small[4:]:
        copy.wait()
    operator = trace_ref[...]
    inverse = inverse_ref[...]
    half = 0.5 * dot_full(inverse, lift_ref[...])
    whole = inverse + dot_full(half, operator)
    at_ref[...] = weights(rows(whole, operator))
    c_ref[...] = weights(rows(whole, operator)[:, 0:NODES])
    b_ref[...] = weights(half)

    flat = stage.reshape(EX // 4 * STATE * 8, 128)

    def begin(c):
        for h in range(2):
            load(c, h).wait()
        for r in range(8):
            x = c * 8 + r
            halves = [flat[row(c, h, r), :] for h in range(2)]
            both = dot(at_ref[...], triple(lanes(*halves)))
            acc_ref[x] = both[0:STATE]
            tr_ref[x] = both[STATE:]

    far = (GX - 1) * (GY - 1)
    share = far // (EX // 8 - 1)

    def begin_and_send(c, carry):
        for u in range(share):
            k = ((c - 1) * share + u) * 52 % far
            send(((px + 1 + k // (GY - 1)) % GX, (py + 1 + k % (GY - 1)) % GY))
        begin(c)
        return carry

    begin(0)
    pl.semaphore_wait(all_in, GY - 1)
    lax.fori_loop(1, EX // 8, begin_and_send, 0)
    rest = pl.ds(0, (DEV - 1) * USED)
    pltpu.make_async_copy(out_ref.at[rest], out_ref.at[rest], far_sem.at[0]).wait()
    pltpu.make_async_copy(got_ref.at[rest], got_ref.at[rest], far_sem.at[1]).wait()
    unpack(got_ref, pay_ref, col_ref, rowid_ref)
    force(0, pay_ref, col_ref, rowid_ref, force_ref)

    peers = (
        (lax.rem(px + GX - 1, GX), py),
        (lax.rem(px + 1, GX), py),
        (px, lax.rem(py + GY - 1, GY)),
        (px, lax.rem(py + 1, GY)),
    )

    def send_halos(s, near_ref, down, up):
        ysend[s, 0] = down
        ysend[s, 1] = up
        pairs = (
            (near_ref.at[0, FN : 2 * FN], near_ref.at[EX, FN : 2 * FN]),
            (near_ref.at[EX + 1, 0:FN], near_ref.at[1, 0:FN]),
            (ysend.at[s, 0], yrecv.at[s, 1]),
            (ysend.at[s, 1], yrecv.at[s, 0]),
        )
        copies = []
        for k in range(4):
            copies.append(
                pltpu.make_async_remote_copy(
                    src_ref=pairs[k][0],
                    dst_ref=pairs[k][1],
                    send_sem=near_send.at[s, k],
                    recv_sem=near_recv.at[s, k],
                    device_id=peers[k],
                    device_id_type=MESH,
                )
            )
            copies[-1].start()
        return copies

    def take_halos(s, near_ref, copies):
        for copy in copies:
            copy.wait()
        below = jnp.where(py == 0, ysend[s, 0], yrecv[s, 0])
        above = jnp.where(py == GY - 1, ysend[s, 1], yrecv[s, 1])
        patch(near_ref, below, above)

    def correct_traces(x, carry):
        tr = dot(c_ref[STATE : STATE + 4 * FN, :], triple(force_ref[0, x]))
        return put(x, tr_ref[x] + tr, near1_ref, carry)

    def correct(x, carry):
        acc_ref[x] += dot(c_ref[0:STATE, :], triple(force_ref[0, x]))
        return carry

    def middle(x, carry):
        value = finish(x, acc_ref, near1_ref, b_ref, scale_ref)
        hi, lo = split(rows(value[0:NODES] + force_ref[1, x], value[NODES:STATE]))
        slab[x, 0:STATE, :] = hi
        slab[x, STATE : 2 * STATE, :] = lo
        return carry

    def trace(x, carry):
        tr = dot(at_ref[STATE : STATE + 4 * FN, :], rows(slab[x], slab[x, 0:STATE, :]))
        return put(x, tr, near2_ref, carry)

    def hold(x, carry):
        acc_ref[x] = dot(at_ref[0:STATE, :], rows(slab[x], slab[x, 0:STATE, :]))
        return carry

    rim = jnp.zeros((FN, 128), F32)
    down, up = lax.fori_loop(0, EX, correct_traces, (rim, rim), unroll=16)
    copies = send_halos(0, near1_ref, down, up)
    lax.fori_loop(0, EX, correct, 0, unroll=16)
    force(1, pay_ref, col_ref, rowid_ref, force_ref)
    take_halos(0, near1_ref, copies)
    lax.fori_loop(0, EX, middle, 0, unroll=16)
    down, up = lax.fori_loop(0, EX, trace, (rim, rim), unroll=16)
    copies = send_halos(1, near2_ref, down, up)
    lax.fori_loop(0, EX, hold, 0, unroll=16)
    take_halos(1, near2_ref, copies)


def last_kernel(acc_ref, near_ref, b_ref, scale_ref, out_ref, stage, sem):
    def store(c, h):
        band = pl.ds(pl.multiple_of(c * 8, 8), 8)
        column = slice(h * 128, h * 128 + 128)
        return pltpu.make_async_copy(
            stage.at[tile(c, h)], out_ref.at[:, band, column], sem.at[c, h]
        )

    flat = stage.reshape(EX // 4 * STATE * 8, 128)

    def body(c, carry):
        for r in range(8):
            value = finish(c * 8 + r, acc_ref, near_ref, b_ref, scale_ref)
            for h in range(2):
                flat[row(c, h, r), :] = value[:, h * 128 : h * 128 + 128]
        for h in range(2):
            store(c, h).start()
        return carry

    lax.fori_loop(0, EX // 8, body, 0)
    for c in range(EX // 8):
        for h in range(2):
            store(c, h).wait()


def local(
    adjoint_state, inverse_scale, element_inverse, trace_op, lift_op,
    obs_elem, obs_count, obs_basis, innovation,
):
    acc, near, lift, scale = pl.pallas_call(
        main_kernel,
        out_shape=(
            pltpu.VMEM((EX, STATE, EY), F32),
            pltpu.VMEM((EX + 2, 4 * FN, EY), F32),
            pltpu.VMEM((STATE, 12 * FN), BF),
            pltpu.VMEM((EX, EY), F32),
        ),
        in_specs=[HBM] * 9,
        out_specs=(VMEM, VMEM, VMEM, VMEM),
        scratch_shapes=[
            pltpu.VMEM((EX // 4 * STATE, 8, 128), F32),
            pltpu.VMEM((EX, 2 * STATE, EY), BF),
            pltpu.VMEM((EX + 2, 4 * FN, EY), F32),
            pltpu.VMEM((EX, 4 * FN, EY), F32),
            pltpu.VMEM((STEPS, EX, NODES, EY), F32),
            pltpu.VMEM((STEPS, NODES, 2 * OBS), BF),
            pltpu.VMEM((STEPS, 2 * OBS, EY), BF),
            pltpu.VMEM((8, OBS), jnp.int32),
            pltpu.VMEM((STATE + 4 * FN, 3 * STATE), BF),
            pltpu.VMEM((STATE + 4 * FN, 3 * NODES), BF),
            pltpu.VMEM((STATE, STATE), F32),
            pltpu.VMEM((4 * FN, STATE), F32),
            pltpu.VMEM((STATE, 4 * FN), F32),
            pltpu.VMEM((STEPS, OBS), jnp.int32),
            pltpu.VMEM((1, STEPS), jnp.int32),
            pltpu.VMEM((STEPS, NODES, OBS), F32),
            pltpu.VMEM((STEPS, OBS), F32),
            pltpu.VMEM((DEV * 8, 128), F32),
            pltpu.VMEM((DEV * 8, 128), F32),
            pltpu.VMEM((STEPS, 2, FN, 128), F32),
            pltpu.VMEM((STEPS, 2, FN, 128), F32),
            pltpu.SemaphoreType.DMA((EX // 8, 2)),
            pltpu.SemaphoreType.DMA((8,)),
            pltpu.SemaphoreType.DMA((2,)),
            pltpu.SemaphoreType.DMA((STEPS, 4)),
            pltpu.SemaphoreType.DMA((STEPS, 4)),
            pltpu.SemaphoreType.REGULAR,
        ],
        compiler_params=pltpu.CompilerParams(
            collective_id=0, has_side_effects=True, vmem_limit_bytes=40 << 20
        ),
        name="main",
    )(
        *(
            pltpu.with_memory_space_constraint(v, pltpu.HBM)
            for v in (
                adjoint_state, inverse_scale, element_inverse, trace_op, lift_op,
                obs_elem, obs_count.T, obs_basis, innovation,
            )
        )
    )
    return pl.pallas_call(
        last_kernel,
        out_shape=jax.ShapeDtypeStruct((STATE, EX, EY), F32),
        in_specs=[VMEM, VMEM, VMEM, VMEM],
        out_specs=HBM,
        scratch_shapes=[
            pltpu.VMEM((EX // 4 * STATE, 8, 128), F32),
            pltpu.SemaphoreType.DMA((EX // 8, 2)),
        ],
        compiler_params=pltpu.CompilerParams(vmem_limit_bytes=24 << 20),
        name="last",
    )(acc, near, lift, scale)


def solution(mesh):
    placed = (
        P(None, "gx", "gy"),
        P("gx", "gy"),
        P(),
        P(),
        P(),
        P(None, ("gx", "gy")),
        P(None, ("gx", "gy")),
        P(None, None, ("gx", "gy")),
        P(None, ("gx", "gy")),
    )
    return jax.shard_map(
        local, mesh=mesh, in_specs=placed, out_specs=P(None, "gx", "gy"), check_vma=False
    )
```

```python
import functools

import jax
import jax.numpy as jnp
from jax import lax
from jax.experimental import pallas as pl
from jax.experimental.pallas import tpu as pltpu
from jax.sharding import PartitionSpec as P

F32 = jnp.float32
BF = jnp.bfloat16
MESH = pl.DeviceIdType.MESH
STEPS = 2
NODES = 64
FN = 24
STATE = 192
EX = 32
EY = 256
OBS = 768
CAP = 6
USED = CAP + 1
GX = 8
GY = 16
DEV = GX * GY
PART = DEV // 2
HOT = PART * CAP
VMEM = pl.BlockSpec(memory_space=pltpu.VMEM)
HBM = pl.BlockSpec(memory_space=pltpu.HBM)


def dot(a, b):
    return jnp.dot(a, b, preferred_element_type=F32)


def rows(*parts):
    return jnp.concatenate(parts, axis=0)


def lanes(*parts):
    return jnp.concatenate(parts, axis=1)


def dot_nt(a, b):
    return lax.dot_general(a, b, (((1,), (1,)), ((), ())), preferred_element_type=F32)


def dot_full(a, b):
    return jnp.dot(a, b, preferred_element_type=F32, precision=lax.Precision.HIGHEST)


def split(v):
    hi = v.astype(BF)
    return hi, (v - hi.astype(F32)).astype(BF)


def triple(v):
    hi, lo = split(v)
    return rows(hi, lo, hi)


def weights(v):
    hi, lo = split(v)
    hi, lo = hi.astype(F32), lo.astype(F32)
    return lanes(hi, hi, lo).astype(BF)


def tile(c, h):
    return pl.ds(pl.multiple_of((c * 2 + h) * STATE, 8), STATE)


def row(c, h, r):
    return pl.ds(pl.multiple_of((c * 2 + h) * STATE * 8, 8) + r, STATE, stride=8)


def iota(shape, dim):
    return lax.broadcasted_iota(jnp.int32, shape, dim)


def pack(elem_ref, count_ref, basis_ref, innov_ref, out_ref):
    lane = iota((1, OBS), 1)
    owner = iota((DEV, OBS), 0)
    tri = (iota((256, 256), 0) < iota((256, 256), 1)).astype(F32).astype(BF)
    row = iota((128, OBS), 0)
    halves = []
    ids = jnp.zeros((DEV, 128), F32)
    for s in range(STEPS):
        elem = elem_ref[s : s + 1, :]
        gx = lax.shift_right_logical(elem, 17)
        lx = lax.shift_right_logical(elem, 12) & (EX - 1)
        gy = lax.shift_right_logical(elem, 8) & (GY - 1)
        ly = elem & (EY - 1)
        live = lane < count_ref[0:1, s : s + 1]
        target = jnp.where(live, gx * GY + gy, -1)
        member = (owner == target).astype(F32)
        carry = jnp.zeros((DEV, 1), F32)
        running = []
        for b in range(OBS // 256):
            part = member[:, b * 256 : (b + 1) * 256]
            running.append(dot(part.astype(BF), tri) + carry)
            carry = carry + jnp.sum(part, axis=1, keepdims=True)
        before = jnp.concatenate(running, axis=1)
        rank = jnp.sum(member * before, axis=0, keepdims=True).astype(jnp.int32)
        hi, lo = split(basis_ref[s] * innov_ref[s : s + 1, :])
        both = jnp.concatenate([hi, lo], axis=0)
        picked = []
        for j in range(CAP):
            chosen = jnp.where(rank == j, member, 0.0).astype(BF)
            got = dot_nt(chosen, both)
            picked.append(got + pltpu.roll(got, 64, 1))
        halves.append(picked)
        where = jnp.where(row == rank + 16 * s, lx + 1, 0)
        where = where + jnp.where(row == rank + 16 * s + 8, ly, 0)
        ids = ids + dot_nt(member.astype(BF), where.astype(F32).astype(BF))
    low = iota((DEV, 128), 1) < 64
    for j in range(CAP):
        out_ref[pl.ds(j, DEV, stride=8), :] = jnp.where(low, halves[0][j], halves[1][j])
    out_ref[pl.ds(CAP, DEV, stride=8), :] = ids


def unpack(part, got_ref, pay_ref, col_ref, rowid_ref):
    def get(j):
        return got_ref[pl.ds(part * PART * 8 + j, PART, stride=8), :]

    low = iota((1, 128), 1) < PART
    ids = rows(get(CAP), get(CAP)).T
    values = [rows(get(j), get(j + 1)).T for j in range(0, CAP, 2)]
    for s in range(STEPS):
        hi, lo = split(lanes(*[v[s * NODES : s * NODES + NODES] for v in values]))
        pay_ref[s, :, 2 * HOT * part : 2 * HOT * part + HOT] = hi
        pay_ref[s, :, 2 * HOT * part + HOT : 2 * HOT * (part + 1)] = lo

        def spread(first):
            at = [ids[first + j : first + j + 1, :] for j in range(CAP)]
            at = [jnp.where(low, at[j], at[j + 1]) for j in range(0, CAP, 2)]
            return lanes(*at).astype(jnp.int32)

        rowid_ref[s : s + 1, HOT * part : HOT * part + HOT] = spread(s * 16) - 1
        hot = (iota((EY, HOT), 0) == spread(s * 16 + 8)).astype(F32).T.astype(BF)
        col_ref[s, 2 * HOT * part : 2 * HOT * part + HOT, :] = hot
        col_ref[s, 2 * HOT * part + HOT : 2 * HOT * (part + 1), :] = hot


def force(s, parts, pay_ref, col_ref, rowid_ref, force_ref):
    group = 16
    start, stop = parts[0], parts[-1] + 1

    def body(g, carry):
        rowid = rowid_ref[s : s + 1, HOT * start : HOT * stop]
        pay = pay_ref[s, :, 2 * HOT * start : 2 * HOT * stop]
        stack = []
        for i in range(group):
            here = (rowid == g * group + i).astype(F32).astype(BF)
            here = [here[:, HOT * p : HOT * p + HOT] for p in range(stop - start)]
            stack.append(pay * lanes(*[here[p // 2] for p in range(2 * len(here))]))
        got = dot(rows(*stack), col_ref[s, 2 * HOT * start : 2 * HOT * stop, :])
        for i in range(group):
            mine = got[i * NODES : i * NODES + NODES]
            if start > 0:
                mine = mine + force_ref[s, g * group + i]
            force_ref[s, g * group + i] = mine
        return carry

    lax.fori_loop(0, EX // group, body, 0)


def put(x, tr, near_ref, carry):
    down, up = carry
    near_ref[x, FN : 2 * FN, :] = tr[0:FN]
    near_ref[x + 2, 0:FN, :] = tr[FN : 2 * FN]
    from_south = pltpu.roll(tr[3 * FN : 4 * FN], 1, 1)
    from_north = pltpu.roll(tr[2 * FN : 3 * FN], EY - 1, 1)
    near_ref[x + 1, 2 * FN : 3 * FN, :] = from_south
    near_ref[x + 1, 3 * FN : 4 * FN, :] = from_north
    here = iota((FN, 128), 1) == x
    up = jnp.where(here, from_south[:, 0:1], up)
    down = jnp.where(here, from_north[:, EY - 1 : EY], down)
    return down, up


def finish(x, acc_ref, near_ref, rim_ref, b_ref, scale_ref):
    lane = iota((FN, 128), 1)
    below = pltpu.roll(rim_ref[0], (128 - x) % 128, 1)
    above = pltpu.roll(rim_ref[1], 127 - x, 1)
    near = near_ref[x + 1]
    south, north = near[2 * FN : 3 * FN], near[3 * FN : 4 * FN]
    south = lanes(jnp.where(lane == 0, below, south[:, 0:128]), south[:, 128:256])
    north = lanes(north[:, 0:128], jnp.where(lane == 127, above, north[:, 128:256]))
    lifted = dot(b_ref[...], triple(rows(near[0 : 2 * FN], south, north)))
    return (acc_ref[x] + lifted) * scale_ref[pl.ds(x, 1), :]


def main_kernel(
    state_hbm, scale_hbm, inverse_hbm, trace_hbm, lift_hbm, elem_hbm, count_hbm, basis_hbm, innov_hbm,
    acc_ref, near2_ref, rim_ref, b_ref, scale_ref,
    stage, slab, near1_ref, tr_ref, force_ref, pay_ref, col_ref, rowid_ref, at_ref, c_ref,
    inverse_ref, trace_ref, lift_ref, elem_ref, count_ref, basis_ref, innov_ref,
    out_ref, got_ref, ysend, yrecv,
    load_sem, small_sem, far_sem, near_send, near_recv, all_in,
):
    px, py = lax.axis_index("gx"), lax.axis_index("gy")
    me = px * GY + py
    barrier = pltpu.get_barrier_semaphore()
    row_peers = [((px + k) % GX, py) for k in range(1, GX)]
    column_peers = [(px, (py + k) % GY) for k in range(1, GY)]
    for peer in row_peers + column_peers:
        pl.semaphore_signal(barrier, inc=1, device_id=peer, device_id_type=MESH)
    small = []
    for k, (src, dst) in enumerate(
        (
            (elem_hbm, elem_ref), (count_hbm, count_ref), (basis_hbm, basis_ref),
            (innov_hbm, innov_ref), (inverse_hbm, inverse_ref), (trace_hbm, trace_ref),
            (lift_hbm, lift_ref), (scale_hbm, scale_ref),
        )
    ):
        small.append(pltpu.make_async_copy(src, dst, small_sem.at[k]))
        small[-1].start()

    def load(c, h):
        column = slice(h * 128, h * 128 + 128)
        band = pl.ds(pl.multiple_of(c * 8, 8), 8)
        return pltpu.make_async_copy(
            state_hbm.at[:, band, column], stage.at[tile(c, h)], load_sem.at[c, h]
        )

    for c in range(EX // 8):
        for h in range(2):
            load(c, h).start()
    for copy in small[0:4]:
        copy.wait()
    pack(elem_ref, count_ref, basis_ref, innov_ref, out_ref)
    mine = pl.ds(pl.multiple_of(me * 8, 8), USED)
    got_ref[0:USED, :] = out_ref[mine, :]
    pl.semaphore_wait(barrier, GX + GY - 2)
    for peer in column_peers:
        pl.semaphore_signal(all_in, inc=1, device_id=peer, device_id_type=MESH)

    def send(peer, slot):
        to = peer[0] * GY + peer[1]
        pltpu.make_async_remote_copy(
            src_ref=out_ref.at[pl.ds(pl.multiple_of(to * 8, 8), USED)],
            dst_ref=got_ref.at[pl.ds(pl.multiple_of(slot * 8, 8), USED)],
            send_sem=far_sem.at[0],
            recv_sem=far_sem.at[1 + slot // PART],
            device_id=peer,
            device_id_type=MESH,
        ).start()

    for k, peer in enumerate(row_peers + column_peers):
        send(peer, k + 1)
    for copy in small[4:]:
        copy.wait()
    operator = trace_ref[...]
    inverse = inverse_ref[...]
    half = 0.5 * dot_full(inverse, lift_ref[...])
    whole = inverse + dot_full(half, operator)
    at_ref[...] = weights(rows(whole, operator))
    c_ref[...] = weights(rows(whole, operator)[:, 0:NODES])
    b_ref[...] = weights(half)

    flat = stage.reshape(EX // 4 * STATE * 8, 128)

    def begin(c):
        for h in range(2):
            load(c, h).wait()
        for r in range(8):
            x = c * 8 + r
            halves = [flat[row(c, h, r), :] for h in range(2)]
            both = dot(at_ref[...], triple(lanes(*halves)))
            acc_ref[x] = both[0:STATE]
            tr_ref[x] = both[STATE:]

    far = (GX - 1) * (GY - 1)
    share = far // (EX // 8 - 1)

    def begin_and_send(c, carry):
        for u in range(share):
            turn = (c - 1) * share + u
            k = turn * 52 % far
            peer = ((px + 1 + k // (GY - 1)) % GX, (py + 1 + k % (GY - 1)) % GY)
            send(peer, GX + GY - 1 + turn)
        begin(c)
        return carry

    begin(0)
    pl.semaphore_wait(all_in, GY - 1)
    lax.fori_loop(1, EX // 8, begin_and_send, 0)
    for part, count in ((0, PART - 1), (1, PART)):
        some = pl.ds(0, count * USED)
        pltpu.make_async_copy(got_ref.at[some], got_ref.at[some], far_sem.at[1 + part]).wait()
        unpack(part, got_ref, pay_ref, col_ref, rowid_ref)
        force(0, (part,), pay_ref, col_ref, rowid_ref, force_ref)

    peers = (
        (lax.rem(px + GX - 1, GX), py),
        (lax.rem(px + 1, GX), py),
        (px, lax.rem(py + GY - 1, GY)),
        (px, lax.rem(py + 1, GY)),
    )

    def send_halos(s, near_ref, down, up):
        ysend[s, 0] = down
        ysend[s, 1] = up
        pairs = (
            (near_ref.at[0, FN : 2 * FN], near_ref.at[EX, FN : 2 * FN]),
            (near_ref.at[EX + 1, 0:FN], near_ref.at[1, 0:FN]),
            (ysend.at[s, 0], yrecv.at[s, 1]),
            (ysend.at[s, 1], yrecv.at[s, 0]),
        )
        copies = []
        for k in range(4):
            copies.append(
                pltpu.make_async_remote_copy(
                    src_ref=pairs[k][0],
                    dst_ref=pairs[k][1],
                    send_sem=near_send.at[s, k],
                    recv_sem=near_recv.at[s, k],
                    device_id=peers[k],
                    device_id_type=MESH,
                )
            )
            copies[-1].start()
        return copies

    def take_halos(s, copies):
        for copy in copies:
            copy.wait()
        rim_ref[0] = jnp.where(py == 0, ysend[s, 0], yrecv[s, 0])
        rim_ref[1] = jnp.where(py == GY - 1, ysend[s, 1], yrecv[s, 1])

    def correct_traces(x, carry):
        tr = dot(c_ref[STATE : STATE + 4 * FN, :], triple(force_ref[0, x]))
        return put(x, tr_ref[x] + tr, near1_ref, carry)

    def correct(x, carry):
        acc_ref[x] += dot(c_ref[0:STATE, :], triple(force_ref[0, x]))
        return carry

    def middle(x, carry):
        value = finish(x, acc_ref, near1_ref, rim_ref, b_ref, scale_ref)
        hi, lo = split(rows(value[0:NODES] + force_ref[1, x], value[NODES:STATE]))
        slab[x, 0:STATE, :] = hi
        slab[x, STATE : 2 * STATE, :] = lo
        return carry

    def trace(x, carry):
        tr = dot(at_ref[STATE : STATE + 4 * FN, :], rows(slab[x], slab[x, 0:STATE, :]))
        return put(x, tr, near2_ref, carry)

    def hold(x, carry):
        acc_ref[x] = dot(at_ref[0:STATE, :], rows(slab[x], slab[x, 0:STATE, :]))
        return carry

    rim = jnp.zeros((FN, 128), F32)
    down, up = lax.fori_loop(0, EX, correct_traces, (rim, rim), unroll=16)
    copies = send_halos(0, near1_ref, down, up)
    lax.fori_loop(0, EX, correct, 0, unroll=16)
    force(1, (0, 1), pay_ref, col_ref, rowid_ref, force_ref)
    take_halos(0, copies)
    lax.fori_loop(0, EX, middle, 0, unroll=16)
    down, up = lax.fori_loop(0, EX, trace, (rim, rim), unroll=16)
    copies = send_halos(1, near2_ref, down, up)
    lax.fori_loop(0, EX, hold, 0, unroll=16)
    take_halos(1, copies)
    rest = pl.ds(0, (DEV - 1) * USED)
    pltpu.make_async_copy(out_ref.at[rest], out_ref.at[rest], far_sem.at[0]).wait()


def last_kernel(acc_ref, near_ref, rim_ref, b_ref, scale_ref, out_ref, stage, sem):
    def store(c, h):
        band = pl.ds(pl.multiple_of(c * 8, 8), 8)
        column = slice(h * 128, h * 128 + 128)
        return pltpu.make_async_copy(
            stage.at[tile(c, h)], out_ref.at[:, band, column], sem.at[c, h]
        )

    flat = stage.reshape(EX // 4 * STATE * 8, 128)

    def body(c, carry):
        for r in range(8):
            value = finish(c * 8 + r, acc_ref, near_ref, rim_ref, b_ref, scale_ref)
            for h in range(2):
                flat[row(c, h, r), :] = value[:, h * 128 : h * 128 + 128]
        for h in range(2):
            store(c, h).start()
        return carry

    lax.fori_loop(0, EX // 8, body, 0)
    for c in range(EX // 8):
        for h in range(2):
            store(c, h).wait()


def local(
    adjoint_state, inverse_scale, element_inverse, trace_op, lift_op,
    obs_elem, obs_count, obs_basis, innovation,
):
    acc, near, rim, lift, scale = pl.pallas_call(
        main_kernel,
        out_shape=(
            pltpu.VMEM((EX, STATE, EY), F32),
            pltpu.VMEM((EX + 2, 4 * FN, EY), F32),
            pltpu.VMEM((2, FN, 128), F32),
            pltpu.VMEM((STATE, 12 * FN), BF),
            pltpu.VMEM((EX, EY), F32),
        ),
        in_specs=[HBM] * 9,
        out_specs=(VMEM,) * 5,
        scratch_shapes=[
            pltpu.VMEM((EX // 4 * STATE, 8, 128), F32),
            pltpu.VMEM((EX, 2 * STATE, EY), BF),
            pltpu.VMEM((EX + 2, 4 * FN, EY), F32),
            pltpu.VMEM((EX, 4 * FN, EY), F32),
            pltpu.VMEM((STEPS, EX, NODES, EY), F32),
            pltpu.VMEM((STEPS, NODES, 2 * OBS), BF),
            pltpu.VMEM((STEPS, 2 * OBS, EY), BF),
            pltpu.VMEM((8, OBS), jnp.int32),
            pltpu.VMEM((STATE + 4 * FN, 3 * STATE), BF),
            pltpu.VMEM((STATE + 4 * FN, 3 * NODES), BF),
            pltpu.VMEM((STATE, STATE), F32),
            pltpu.VMEM((4 * FN, STATE), F32),
            pltpu.VMEM((STATE, 4 * FN), F32),
            pltpu.VMEM((STEPS, OBS), jnp.int32),
            pltpu.VMEM((1, STEPS), jnp.int32),
            pltpu.VMEM((STEPS, NODES, OBS), F32),
            pltpu.VMEM((STEPS, OBS), F32),
            pltpu.VMEM((DEV * 8, 128), F32),
            pltpu.VMEM((DEV * 8, 128), F32),
            pltpu.VMEM((STEPS, 2, FN, 128), F32),
            pltpu.VMEM((STEPS, 2, FN, 128), F32),
            pltpu.SemaphoreType.DMA((EX // 8, 2)),
            pltpu.SemaphoreType.DMA((8,)),
            pltpu.SemaphoreType.DMA((3,)),
            pltpu.SemaphoreType.DMA((STEPS, 4)),
            pltpu.SemaphoreType.DMA((STEPS, 4)),
            pltpu.SemaphoreType.REGULAR,
        ],
        compiler_params=pltpu.CompilerParams(
            collective_id=0, has_side_effects=True, vmem_limit_bytes=40 << 20
        ),
        name="main",
    )(
        *(
            pltpu.with_memory_space_constraint(v, pltpu.HBM)
            for v in (
                adjoint_state, inverse_scale, element_inverse, trace_op, lift_op,
                obs_elem, obs_count.T, obs_basis, innovation,
            )
        )
    )
    return pl.pallas_call(
        last_kernel,
        out_shape=jax.ShapeDtypeStruct((STATE, EX, EY), F32),
        in_specs=[VMEM] * 5,
        out_specs=HBM,
        scratch_shapes=[
            pltpu.VMEM((EX // 4 * STATE, 8, 128), F32),
            pltpu.SemaphoreType.DMA((EX // 8, 2)),
        ],
        compiler_params=pltpu.CompilerParams(vmem_limit_bytes=24 << 20),
        name="last",
    )(acc, near, rim, lift, scale)


def solution(mesh):
    placed = (
        P(None, "gx", "gy"),
        P("gx", "gy"),
        P(),
        P(),
        P(),
        P(None, ("gx", "gy")),
        P(None, ("gx", "gy")),
        P(None, None, ("gx", "gy")),
        P(None, ("gx", "gy")),
    )
    return jax.shard_map(
        local, mesh=mesh, in_specs=placed, out_specs=P(None, "gx", "gy"), check_vma=False
    )
```

```python
import functools

import jax
import jax.numpy as jnp
from jax import lax
from jax.experimental import pallas as pl
from jax.experimental.pallas import tpu as pltpu
from jax.sharding import PartitionSpec as P

F32 = jnp.float32
BF = jnp.bfloat16
MESH = pl.DeviceIdType.MESH
STEPS = 2
NODES = 64
FN = 24
STATE = 192
EX = 32
EY = 256
OBS = 768
CAP = 6
USED = CAP + 1
GX = 8
GY = 16
DEV = GX * GY
PART = DEV // 2
HOT = PART * CAP
VMEM = pl.BlockSpec(memory_space=pltpu.VMEM)
HBM = pl.BlockSpec(memory_space=pltpu.HBM)


def dot(a, b):
    return jnp.dot(a, b, preferred_element_type=F32)


def rows(*parts):
    return jnp.concatenate(parts, axis=0)


def lanes(*parts):
    return jnp.concatenate(parts, axis=1)


def dot_nt(a, b):
    return lax.dot_general(a, b, (((1,), (1,)), ((), ())), preferred_element_type=F32)


def dot_full(a, b):
    return jnp.dot(a, b, preferred_element_type=F32, precision=lax.Precision.HIGHEST)


def split(v):
    hi = v.astype(BF)
    return hi, (v - hi.astype(F32)).astype(BF)


def triple(v):
    hi, lo = split(v)
    return rows(hi, lo, hi)


def weights(*values):
    parts = []
    for v in values:
        hi, lo = split(v)
        hi, lo = hi.astype(F32), lo.astype(F32)
        parts += [hi, hi, lo]
    return lanes(*parts).astype(BF)


def tile(c, h):
    return pl.ds(pl.multiple_of((c * 2 + h) * STATE, 8), STATE)


def row(c, h, r):
    return pl.ds(pl.multiple_of((c * 2 + h) * STATE * 8, 8) + r, STATE, stride=8)


def iota(shape, dim):
    return lax.broadcasted_iota(jnp.int32, shape, dim)


def pack(elem_ref, count_ref, basis_ref, innov_ref, out_ref):
    lane = iota((1, OBS), 1)
    owner = iota((DEV, OBS), 0)
    tri = (iota((256, 256), 0) < iota((256, 256), 1)).astype(F32).astype(BF)
    row = iota((128, OBS), 0)
    halves = []
    ids = jnp.zeros((DEV, 128), F32)
    for s in range(STEPS):
        elem = elem_ref[s : s + 1, :]
        gx = lax.shift_right_logical(elem, 17)
        lx = lax.shift_right_logical(elem, 12) & (EX - 1)
        gy = lax.shift_right_logical(elem, 8) & (GY - 1)
        ly = elem & (EY - 1)
        live = lane < count_ref[0:1, s : s + 1]
        target = jnp.where(live, gx * GY + gy, -1)
        member = (owner == target).astype(F32)
        carry = jnp.zeros((DEV, 1), F32)
        running = []
        for b in range(OBS // 256):
            part = member[:, b * 256 : (b + 1) * 256]
            running.append(dot(part.astype(BF), tri) + carry)
            carry = carry + jnp.sum(part, axis=1, keepdims=True)
        before = jnp.concatenate(running, axis=1)
        rank = jnp.sum(member * before, axis=0, keepdims=True).astype(jnp.int32)
        hi, lo = split(basis_ref[s] * innov_ref[s : s + 1, :])
        both = jnp.concatenate([hi, lo], axis=0)
        picked = []
        for j in range(CAP):
            chosen = jnp.where(rank == j, member, 0.0).astype(BF)
            got = dot_nt(chosen, both)
            picked.append(got + pltpu.roll(got, 64, 1))
        halves.append(picked)
        where = jnp.where(row == rank + 16 * s, lx + 1, 0)
        where = where + jnp.where(row == rank + 16 * s + 8, ly, 0)
        ids = ids + dot_nt(member.astype(BF), where.astype(F32).astype(BF))
    low = iota((DEV, 128), 1) < 64
    for j in range(CAP):
        out_ref[pl.ds(j, DEV, stride=8), :] = jnp.where(low, halves[0][j], halves[1][j])
    out_ref[pl.ds(CAP, DEV, stride=8), :] = ids


def unpack(part, got_ref, pay_ref, col_ref, rowid_ref):
    def get(j):
        return got_ref[pl.ds(part * PART * 8 + j, PART, stride=8), :]

    low = iota((1, 128), 1) < PART
    ids = rows(get(CAP), get(CAP)).T
    values = [rows(get(j), get(j + 1)).T for j in range(0, CAP, 2)]
    for s in range(STEPS):
        hi, lo = split(lanes(*[v[s * NODES : s * NODES + NODES] for v in values]))
        pay_ref[s, :, 2 * HOT * part : 2 * HOT * part + HOT] = hi
        pay_ref[s, :, 2 * HOT * part + HOT : 2 * HOT * (part + 1)] = lo

        def spread(first):
            at = [ids[first + j : first + j + 1, :] for j in range(CAP)]
            at = [jnp.where(low, at[j], at[j + 1]) for j in range(0, CAP, 2)]
            return lanes(*at).astype(jnp.int32)

        rowid_ref[s : s + 1, HOT * part : HOT * part + HOT] = spread(s * 16) - 1
        hot = (iota((EY, HOT), 0) == spread(s * 16 + 8)).astype(F32).T.astype(BF)
        col_ref[s, 2 * HOT * part : 2 * HOT * part + HOT, :] = hot
        col_ref[s, 2 * HOT * part + HOT : 2 * HOT * (part + 1), :] = hot


def force(s, parts, pay_ref, col_ref, rowid_ref, force_ref):
    group = 16
    start, stop = parts[0], parts[-1] + 1

    def body(g, carry):
        rowid = rowid_ref[s : s + 1, HOT * start : HOT * stop]
        pay = pay_ref[s, :, 2 * HOT * start : 2 * HOT * stop]
        stack = []
        for i in range(group):
            here = (rowid == g * group + i).astype(F32).astype(BF)
            here = [here[:, HOT * p : HOT * p + HOT] for p in range(stop - start)]
            stack.append(pay * lanes(*[here[p // 2] for p in range(2 * len(here))]))
        got = dot(rows(*stack), col_ref[s, 2 * HOT * start : 2 * HOT * stop, :])
        for i in range(group):
            mine = got[i * NODES : i * NODES + NODES]
            if start > 0:
                mine = mine + force_ref[s, g * group + i]
            force_ref[s, g * group + i] = mine
        return carry

    lax.fori_loop(0, EX // group, body, 0)


def put(x, tr, near_ref, carry):
    down, up = carry
    near_ref[x, FN : 2 * FN, :] = tr[0:FN]
    near_ref[x + 2, 0:FN, :] = tr[FN : 2 * FN]
    from_south = pltpu.roll(tr[3 * FN : 4 * FN], 1, 1)
    from_north = pltpu.roll(tr[2 * FN : 3 * FN], EY - 1, 1)
    near_ref[x + 1, 2 * FN : 3 * FN, :] = from_south
    near_ref[x + 1, 3 * FN : 4 * FN, :] = from_north
    here = iota((FN, 128), 1) == x
    up = jnp.where(here, from_south[:, 0:1], up)
    down = jnp.where(here, from_north[:, EY - 1 : EY], down)
    return down, up


def finish(x, acc_ref, near_ref, rim_ref, b_ref, scale_ref, force=None):
    lane = iota((FN, 128), 1)
    below = pltpu.roll(rim_ref[0], (128 - x) % 128, 1)
    above = pltpu.roll(rim_ref[1], 127 - x, 1)
    near = near_ref[x + 1]
    south, north = near[2 * FN : 3 * FN], near[3 * FN : 4 * FN]
    south = lanes(jnp.where(lane == 0, below, south[:, 0:128]), south[:, 128:256])
    north = lanes(north[:, 0:128], jnp.where(lane == 127, above, north[:, 128:256]))
    given = triple(rows(near[0 : 2 * FN], south, north))
    if force is not None:
        given = rows(given, triple(force))
    lifted = dot(b_ref[...], given)
    return (acc_ref[x] + lifted) * scale_ref[pl.ds(x, 1), :]


def main_kernel(
    state_hbm, scale_hbm, inverse_hbm, trace_hbm, lift_hbm, elem_hbm, count_hbm, basis_hbm, innov_hbm,
    acc_ref, near2_ref, rim_ref, b_ref, scale_ref,
    stage, slab, near1_ref, tr_ref, force_ref, pay_ref, col_ref, rowid_ref, at_ref, c_ref, bc_ref, t_ref,
    inverse_ref, trace_ref, lift_ref, elem_ref, count_ref, basis_ref, innov_ref,
    out_ref, got_ref, ysend, yrecv,
    load_sem, small_sem, far_sem, near_send, near_recv, all_in,
):
    px, py = lax.axis_index("gx"), lax.axis_index("gy")
    me = px * GY + py
    barrier = pltpu.get_barrier_semaphore()
    row_peers = [((px + k) % GX, py) for k in range(1, GX)]
    column_peers = [(px, (py + k) % GY) for k in range(1, GY)]
    for peer in row_peers + column_peers:
        pl.semaphore_signal(barrier, inc=1, device_id=peer, device_id_type=MESH)
    small = []
    for k, (src, dst) in enumerate(
        (
            (elem_hbm, elem_ref), (count_hbm, count_ref), (basis_hbm, basis_ref),
            (innov_hbm, innov_ref), (inverse_hbm, inverse_ref), (trace_hbm, trace_ref),
            (lift_hbm, lift_ref), (scale_hbm, scale_ref),
        )
    ):
        small.append(pltpu.make_async_copy(src, dst, small_sem.at[k]))
        small[-1].start()

    def load(c, h):
        column = slice(h * 128, h * 128 + 128)
        band = pl.ds(pl.multiple_of(c * 8, 8), 8)
        return pltpu.make_async_copy(
            state_hbm.at[:, band, column], stage.at[tile(c, h)], load_sem.at[c, h]
        )

    for c in range(EX // 8):
        for h in range(2):
            load(c, h).start()
    for copy in small[0:4]:
        copy.wait()
    pack(elem_ref, count_ref, basis_ref, innov_ref, out_ref)
    mine = pl.ds(pl.multiple_of(me * 8, 8), USED)
    got_ref[0:USED, :] = out_ref[mine, :]
    pl.semaphore_wait(barrier, GX + GY - 2)
    for peer in column_peers:
        pl.semaphore_signal(all_in, inc=1, device_id=peer, device_id_type=MESH)

    def send(peer, slot):
        to = peer[0] * GY + peer[1]
        pltpu.make_async_remote_copy(
            src_ref=out_ref.at[pl.ds(pl.multiple_of(to * 8, 8), USED)],
            dst_ref=got_ref.at[pl.ds(pl.multiple_of(slot * 8, 8), USED)],
            send_sem=far_sem.at[0],
            recv_sem=far_sem.at[1 + slot // PART],
            device_id=peer,
            device_id_type=MESH,
        ).start()

    for k, peer in enumerate(row_peers + column_peers):
        send(peer, k + 1)
    for copy in small[4:]:
        copy.wait()
    operator = trace_ref[...]
    inverse = inverse_ref[...]
    half = 0.5 * dot_full(inverse, lift_ref[...])
    whole = inverse + dot_full(half, operator)
    at_ref[...] = weights(rows(whole, operator))
    c_ref[...] = weights(operator[:, 0:NODES])
    bc_ref[...] = weights(half, whole[:, 0:NODES])
    hi, lo = split(operator)
    t_ref[0 : 4 * FN, :] = hi
    t_ref[4 * FN : 8 * FN, :] = lo
    b_ref[...] = weights(half)

    flat = stage.reshape(EX // 4 * STATE * 8, 128)

    def begin(c):
        for h in range(2):
            load(c, h).wait()
        for r in range(8):
            x = c * 8 + r
            halves = [flat[row(c, h, r), :] for h in range(2)]
            both = dot(at_ref[...], triple(lanes(*halves)))
            acc_ref[x] = both[0:STATE]
            tr_ref[x] = both[STATE:]

    far = (GX - 1) * (GY - 1)
    share = far // (EX // 8 - 1)

    def begin_and_send(c, carry):
        for u in range(share):
            turn = (c - 1) * share + u
            k = turn * 52 % far
            peer = ((px + 1 + k // (GY - 1)) % GX, (py + 1 + k % (GY - 1)) % GY)
            send(peer, GX + GY - 1 + turn)
        begin(c)
        return carry

    begin(0)
    pl.semaphore_wait(all_in, GY - 1)
    lax.fori_loop(1, EX // 8, begin_and_send, 0)
    for part, count in ((0, PART - 1), (1, PART)):
        some = pl.ds(0, count * USED)
        pltpu.make_async_copy(got_ref.at[some], got_ref.at[some], far_sem.at[1 + part]).wait()
        unpack(part, got_ref, pay_ref, col_ref, rowid_ref)
        force(0, (part,), pay_ref, col_ref, rowid_ref, force_ref)

    peers = (
        (lax.rem(px + GX - 1, GX), py),
        (lax.rem(px + 1, GX), py),
        (px, lax.rem(py + GY - 1, GY)),
        (px, lax.rem(py + 1, GY)),
    )

    def send_halos(s, near_ref, down, up):
        ysend[s, 0] = down
        ysend[s, 1] = up
        pairs = (
            (near_ref.at[0, FN : 2 * FN], near_ref.at[EX, FN : 2 * FN]),
            (near_ref.at[EX + 1, 0:FN], near_ref.at[1, 0:FN]),
            (ysend.at[s, 0], yrecv.at[s, 1]),
            (ysend.at[s, 1], yrecv.at[s, 0]),
        )
        copies = []
        for k in range(4):
            copies.append(
                pltpu.make_async_remote_copy(
                    src_ref=pairs[k][0],
                    dst_ref=pairs[k][1],
                    send_sem=near_send.at[s, k],
                    recv_sem=near_recv.at[s, k],
                    device_id=peers[k],
                    device_id_type=MESH,
                )
            )
            copies[-1].start()
        return copies

    def take_halos(s, copies):
        for copy in copies:
            copy.wait()
        rim_ref[0] = jnp.where(py == 0, ysend[s, 0], yrecv[s, 0])
        rim_ref[1] = jnp.where(py == GY - 1, ysend[s, 1], yrecv[s, 1])

    def correct_traces(x, carry):
        tr = dot(c_ref[...], triple(force_ref[0, x]))
        return put(x, tr_ref[x] + tr, near1_ref, carry)

    def middle(x, carry):
        value = finish(
            x, acc_ref, near1_ref, rim_ref, bc_ref, scale_ref, force_ref[0, x]
        )
        hi, lo = split(rows(value[0:NODES] + force_ref[1, x], value[NODES:STATE]))
        slab[x, 0:STATE, :] = hi
        slab[x, STATE : 2 * STATE, :] = lo
        return carry

    def trace(x, carry):
        both = dot(t_ref[...], slab[x, 0:STATE, :])
        tr = dot(t_ref[0 : 4 * FN, :], slab[x, STATE : 2 * STATE, :])
        return put(x, both[0 : 4 * FN] + both[4 * FN : 8 * FN] + tr, near2_ref, carry)

    def hold(x, carry):
        acc_ref[x] = dot(at_ref[0:STATE, :], rows(slab[x], slab[x, 0:STATE, :]))
        return carry

    rim = jnp.zeros((FN, 128), F32)
    down, up = lax.fori_loop(0, EX, correct_traces, (rim, rim), unroll=32)
    copies = send_halos(0, near1_ref, down, up)
    force(1, (0, 1), pay_ref, col_ref, rowid_ref, force_ref)
    take_halos(0, copies)
    lax.fori_loop(0, EX, middle, 0, unroll=32)
    down, up = lax.fori_loop(0, EX, trace, (rim, rim), unroll=32)
    copies = send_halos(1, near2_ref, down, up)
    lax.fori_loop(0, EX, hold, 0, unroll=32)
    take_halos(1, copies)
    rest = pl.ds(0, (DEV - 1) * USED)
    pltpu.make_async_copy(out_ref.at[rest], out_ref.at[rest], far_sem.at[0]).wait()


def last_kernel(acc_ref, near_ref, rim_ref, b_ref, scale_ref, out_ref, stage, sem):
    def store(c, h):
        band = pl.ds(pl.multiple_of(c * 8, 8), 8)
        column = slice(h * 128, h * 128 + 128)
        return pltpu.make_async_copy(
            stage.at[tile(c, h)], out_ref.at[:, band, column], sem.at[c, h]
        )

    flat = stage.reshape(EX // 4 * STATE * 8, 128)

    def body(c, carry):
        for r in range(8):
            value = finish(c * 8 + r, acc_ref, near_ref, rim_ref, b_ref, scale_ref)
            for h in range(2):
                flat[row(c, h, r), :] = value[:, h * 128 : h * 128 + 128]
        for h in range(2):
            store(c, h).start()
        return carry

    lax.fori_loop(0, EX // 8, body, 0)
    for c in range(EX // 8):
        for h in range(2):
            store(c, h).wait()


def local(
    adjoint_state, inverse_scale, element_inverse, trace_op, lift_op,
    obs_elem, obs_count, obs_basis, innovation,
):
    acc, near, rim, lift, scale = pl.pallas_call(
        main_kernel,
        out_shape=(
            pltpu.VMEM((EX, STATE, EY), F32),
            pltpu.VMEM((EX + 2, 4 * FN, EY), F32),
            pltpu.VMEM((2, FN, 128), F32),
            pltpu.VMEM((STATE, 12 * FN), BF),
            pltpu.VMEM((EX, EY), F32),
        ),
        in_specs=[HBM] * 9,
        out_specs=(VMEM,) * 5,
        scratch_shapes=[
            pltpu.VMEM((EX // 4 * STATE, 8, 128), F32),
            pltpu.VMEM((EX, 2 * STATE, EY), BF),
            pltpu.VMEM((EX + 2, 4 * FN, EY), F32),
            pltpu.VMEM((EX, 4 * FN, EY), F32),
            pltpu.VMEM((STEPS, EX, NODES, EY), F32),
            pltpu.VMEM((STEPS, NODES, 2 * OBS), BF),
            pltpu.VMEM((STEPS, 2 * OBS, EY), BF),
            pltpu.VMEM((8, OBS), jnp.int32),
            pltpu.VMEM((STATE + 4 * FN, 3 * STATE), BF),
            pltpu.VMEM((4 * FN, 3 * NODES), BF),
            pltpu.VMEM((STATE, 12 * FN + 3 * NODES), BF),
            pltpu.VMEM((8 * FN, STATE), BF),
            pltpu.VMEM((STATE, STATE), F32),
            pltpu.VMEM((4 * FN, STATE), F32),
            pltpu.VMEM((STATE, 4 * FN), F32),
            pltpu.VMEM((STEPS, OBS), jnp.int32),
            pltpu.VMEM((1, STEPS), jnp.int32),
            pltpu.VMEM((STEPS, NODES, OBS), F32),
            pltpu.VMEM((STEPS, OBS), F32),
            pltpu.VMEM((DEV * 8, 128), F32),
            pltpu.VMEM((DEV * 8, 128), F32),
            pltpu.VMEM((STEPS, 2, FN, 128), F32),
            pltpu.VMEM((STEPS, 2, FN, 128), F32),
            pltpu.SemaphoreType.DMA((EX // 8, 2)),
            pltpu.SemaphoreType.DMA((8,)),
            pltpu.SemaphoreType.DMA((3,)),
            pltpu.SemaphoreType.DMA((STEPS, 4)),
            pltpu.SemaphoreType.DMA((STEPS, 4)),
            pltpu.SemaphoreType.REGULAR,
        ],
        compiler_params=pltpu.CompilerParams(
            collective_id=0, has_side_effects=True, vmem_limit_bytes=40 << 20
        ),
        name="main",
    )(
        *(
            pltpu.with_memory_space_constraint(v, pltpu.HBM)
            for v in (
                adjoint_state, inverse_scale, element_inverse, trace_op, lift_op,
                obs_elem, obs_count.T, obs_basis, innovation,
            )
        )
    )
    return pl.pallas_call(
        last_kernel,
        out_shape=jax.ShapeDtypeStruct((STATE, EX, EY), F32),
        in_specs=[VMEM] * 5,
        out_specs=HBM,
        scratch_shapes=[
            pltpu.VMEM((EX // 4 * STATE, 8, 128), F32),
            pltpu.SemaphoreType.DMA((EX // 8, 2)),
        ],
        compiler_params=pltpu.CompilerParams(vmem_limit_bytes=24 << 20),
        name="last",
    )(acc, near, rim, lift, scale)


def solution(mesh):
    placed = (
        P(None, "gx", "gy"),
        P("gx", "gy"),
        P(),
        P(),
        P(),
        P(None, ("gx", "gy")),
        P(None, ("gx", "gy")),
        P(None, None, ("gx", "gy")),
        P(None, ("gx", "gy")),
    )
    return jax.shard_map(
        local, mesh=mesh, in_specs=placed, out_specs=P(None, "gx", "gy"), check_vma=False
    )
```

```python
import functools

import jax
import jax.numpy as jnp
from jax import lax
from jax.experimental import pallas as pl
from jax.experimental.pallas import tpu as pltpu
from jax.sharding import PartitionSpec as P

F32 = jnp.float32
BF = jnp.bfloat16
MESH = pl.DeviceIdType.MESH
STEPS = 2
NODES = 64
FN = 24
STATE = 192
EX = 32
EY = 256
OBS = 768
CAP = 6
USED = CAP + 1
GX = 8
GY = 16
DEV = GX * GY
PART = DEV // 2
HOT = PART * CAP
VMEM = pl.BlockSpec(memory_space=pltpu.VMEM)
HBM = pl.BlockSpec(memory_space=pltpu.HBM)


def dot(a, b):
    return jnp.dot(a, b, preferred_element_type=F32)


def rows(*parts):
    return jnp.concatenate(parts, axis=0)


def lanes(*parts):
    return jnp.concatenate(parts, axis=1)


def dot_nt(a, b):
    return lax.dot_general(a, b, (((1,), (1,)), ((), ())), preferred_element_type=F32)


def dot_full(a, b):
    return jnp.dot(a, b, preferred_element_type=F32, precision=lax.Precision.HIGHEST)


def split(v):
    hi = v.astype(BF)
    return hi, (v - hi.astype(F32)).astype(BF)


def triple(v):
    hi, lo = split(v)
    return rows(hi, lo, hi)


def weights(*values):
    parts = []
    for v in values:
        hi, lo = split(v)
        hi, lo = hi.astype(F32), lo.astype(F32)
        parts += [hi, hi, lo]
    return lanes(*parts).astype(BF)


def tile(c, h):
    return pl.ds(pl.multiple_of((c * 2 + h) * STATE, 8), STATE)


def row(c, h, r):
    return pl.ds(pl.multiple_of((c * 2 + h) * STATE * 8, 8) + r, STATE, stride=8)


def iota(shape, dim):
    return lax.broadcasted_iota(jnp.int32, shape, dim)


def pack(elem_ref, count_ref, basis_ref, innov_ref, out_ref):
    lane = iota((1, OBS), 1)
    owner = iota((DEV, OBS), 0)
    tri = (iota((256, 256), 0) < iota((256, 256), 1)).astype(F32).astype(BF)
    row = iota((128, OBS), 0)
    halves = []
    ids = jnp.zeros((DEV, 128), F32)
    for s in range(STEPS):
        elem = elem_ref[s : s + 1, :]
        gx = lax.shift_right_logical(elem, 17)
        lx = lax.shift_right_logical(elem, 12) & (EX - 1)
        gy = lax.shift_right_logical(elem, 8) & (GY - 1)
        ly = elem & (EY - 1)
        live = lane < count_ref[0:1, s : s + 1]
        target = jnp.where(live, gx * GY + gy, -1)
        member = (owner == target).astype(F32)
        carry = jnp.zeros((DEV, 1), F32)
        running = []
        for b in range(OBS // 256):
            part = member[:, b * 256 : (b + 1) * 256]
            running.append(dot(part.astype(BF), tri) + carry)
            carry = carry + jnp.sum(part, axis=1, keepdims=True)
        before = jnp.concatenate(running, axis=1)
        rank = jnp.sum(member * before, axis=0, keepdims=True).astype(jnp.int32)
        hi, lo = split(basis_ref[s] * innov_ref[s : s + 1, :])
        both = jnp.concatenate([hi, lo], axis=0)
        picked = []
        for j in range(CAP):
            chosen = jnp.where(rank == j, member, 0.0).astype(BF)
            got = dot_nt(chosen, both)
            picked.append(got + pltpu.roll(got, 64, 1))
        halves.append(picked)
        where = jnp.where(row == rank + 16 * s, lx + 1, 0)
        where = where + jnp.where(row == rank + 16 * s + 8, ly, 0)
        ids = ids + dot_nt(member.astype(BF), where.astype(F32).astype(BF))
    low = iota((DEV, 128), 1) < 64
    for j in range(CAP):
        out_ref[pl.ds(j, DEV, stride=8), :] = jnp.where(low, halves[0][j], halves[1][j])
    out_ref[pl.ds(CAP, DEV, stride=8), :] = ids


def unpack(part, got_ref, pay_ref, col_ref, rowid_ref):
    def get(j):
        return got_ref[pl.ds(part * PART * 8 + j, PART, stride=8), :]

    low = iota((1, 128), 1) < PART
    ids = rows(get(CAP), get(CAP)).T
    values = [rows(get(j), get(j + 1)).T for j in range(0, CAP, 2)]
    for s in range(STEPS):
        hi, lo = split(lanes(*[v[s * NODES : s * NODES + NODES] for v in values]))
        pay_ref[s, :, 2 * HOT * part : 2 * HOT * part + HOT] = hi
        pay_ref[s, :, 2 * HOT * part + HOT : 2 * HOT * (part + 1)] = lo

        def spread(first):
            at = [ids[first + j : first + j + 1, :] for j in range(CAP)]
            at = [jnp.where(low, at[j], at[j + 1]) for j in range(0, CAP, 2)]
            return lanes(*at).astype(jnp.int32)

        rowid_ref[s : s + 1, HOT * part : HOT * part + HOT] = spread(s * 16) - 1
        hot = (iota((EY, HOT), 0) == spread(s * 16 + 8)).astype(F32).T.astype(BF)
        col_ref[s, 2 * HOT * part : 2 * HOT * part + HOT, :] = hot
        col_ref[s, 2 * HOT * part + HOT : 2 * HOT * (part + 1), :] = hot


def force(s, parts, pay_ref, col_ref, rowid_ref, force_ref):
    group = 16
    start, stop = parts[0], parts[-1] + 1

    def body(g, carry):
        rowid = rowid_ref[s : s + 1, HOT * start : HOT * stop]
        pay = pay_ref[s, :, 2 * HOT * start : 2 * HOT * stop]
        stack = []
        for i in range(group):
            here = (rowid == g * group + i).astype(F32).astype(BF)
            here = [here[:, HOT * p : HOT * p + HOT] for p in range(stop - start)]
            stack.append(pay * lanes(*[here[p // 2] for p in range(2 * len(here))]))
        got = dot(rows(*stack), col_ref[s, 2 * HOT * start : 2 * HOT * stop, :])
        for i in range(group):
            mine = got[i * NODES : i * NODES + NODES]
            if start > 0:
                mine = mine + force_ref[s, g * group + i]
            force_ref[s, g * group + i] = mine
        return carry

    lax.fori_loop(0, EX // group, body, 0)


def put(x, tr, near_ref, carry):
    down, up = carry
    near_ref[x, FN : 2 * FN, :] = tr[0:FN]
    near_ref[x + 2, 0:FN, :] = tr[FN : 2 * FN]
    from_south = pltpu.roll(tr[3 * FN : 4 * FN], 1, 1)
    from_north = pltpu.roll(tr[2 * FN : 3 * FN], EY - 1, 1)
    near_ref[x + 1, 2 * FN : 3 * FN, :] = from_south
    near_ref[x + 1, 3 * FN : 4 * FN, :] = from_north
    here = iota((FN, 128), 1) == x
    up = jnp.where(here, from_south[:, 0:1], up)
    down = jnp.where(here, from_north[:, EY - 1 : EY], down)
    return down, up


def finish(x, acc_ref, near_ref, rim_ref, b_ref, scale_ref, force=None):
    lane = iota((FN, 128), 1)
    below = pltpu.roll(rim_ref[0], (128 - x) % 128, 1)
    above = pltpu.roll(rim_ref[1], 127 - x, 1)
    near = near_ref[x + 1]
    south, north = near[2 * FN : 3 * FN], near[3 * FN : 4 * FN]
    south = lanes(jnp.where(lane == 0, below, south[:, 0:128]), south[:, 128:256])
    north = lanes(north[:, 0:128], jnp.where(lane == 127, above, north[:, 128:256]))
    given = triple(rows(near[0 : 2 * FN], south, north))
    if force is not None:
        given = rows(given, triple(force))
    lifted = dot(b_ref[...], given)
    return (acc_ref[x] + lifted) * scale_ref[pl.ds(x, 1), :]


def main_kernel(
    state_hbm, scale_hbm, inverse_hbm, trace_hbm, lift_hbm, elem_hbm, count_hbm, basis_hbm, innov_hbm,
    acc_ref, near2_ref, rim_ref, b_ref, scale_ref,
    stage, slab, near1_ref, tr_ref, force_ref, pay_ref, col_ref, rowid_ref, at_ref, c_ref, bc_ref, t_ref,
    inverse_ref, trace_ref, lift_ref, elem_ref, count_ref, basis_ref, innov_ref,
    out_ref, got_ref, ysend, yrecv,
    load_sem, small_sem, far_sem, near_send, near_recv, all_in,
):
    px, py = lax.axis_index("gx"), lax.axis_index("gy")
    me = px * GY + py
    barrier = pltpu.get_barrier_semaphore()
    row_peers = [((px + k) % GX, py) for k in range(1, GX)]
    column_peers = [(px, (py + k) % GY) for k in range(1, GY)]
    for peer in row_peers + column_peers:
        pl.semaphore_signal(barrier, inc=1, device_id=peer, device_id_type=MESH)
    small = []
    for k, (src, dst) in enumerate(
        (
            (elem_hbm, elem_ref), (count_hbm, count_ref), (basis_hbm, basis_ref),
            (innov_hbm, innov_ref), (inverse_hbm, inverse_ref), (trace_hbm, trace_ref),
            (lift_hbm, lift_ref), (scale_hbm, scale_ref),
        )
    ):
        small.append(pltpu.make_async_copy(src, dst, small_sem.at[k]))
        small[-1].start()

    def load(c, h):
        column = slice(h * 128, h * 128 + 128)
        band = pl.ds(pl.multiple_of(c * 8, 8), 8)
        return pltpu.make_async_copy(
            state_hbm.at[:, band, column], stage.at[tile(c, h)], load_sem.at[c, h]
        )

    for c in range(EX // 8):
        for h in range(2):
            load(c, h).start()
    for copy in small[0:4]:
        copy.wait()
    pack(elem_ref, count_ref, basis_ref, innov_ref, out_ref)
    mine = pl.ds(pl.multiple_of(me * 8, 8), USED)
    got_ref[0:USED, :] = out_ref[mine, :]
    pl.semaphore_wait(barrier, GX + GY - 2)
    for peer in column_peers:
        pl.semaphore_signal(all_in, inc=1, device_id=peer, device_id_type=MESH)

    def send(peer, slot):
        to = peer[0] * GY + peer[1]
        pltpu.make_async_remote_copy(
            src_ref=out_ref.at[pl.ds(pl.multiple_of(to * 8, 8), USED)],
            dst_ref=got_ref.at[pl.ds(pl.multiple_of(slot * 8, 8), USED)],
            send_sem=far_sem.at[0],
            recv_sem=far_sem.at[1 + slot // PART],
            device_id=peer,
            device_id_type=MESH,
        ).start()

    for k, peer in enumerate(row_peers + column_peers):
        send(peer, k + 1)
    for copy in small[4:]:
        copy.wait()
    operator = trace_ref[...]
    inverse = inverse_ref[...]
    half = 0.5 * dot_full(inverse, lift_ref[...])
    whole = inverse + dot_full(half, operator)
    at_ref[...] = weights(rows(whole, operator))
    c_ref[...] = weights(operator[:, 0:NODES])
    bc_ref[...] = weights(half, whole[:, 0:NODES])
    hi, lo = split(operator)
    t_ref[0 : 4 * FN, :] = hi
    t_ref[4 * FN : 8 * FN, :] = lo
    b_ref[...] = weights(half)

    flat = stage.reshape(EX // 4 * STATE * 8, 128)

    def begin(c):
        for h in range(2):
            load(c, h).wait()
        for r in range(8):
            x = c * 8 + r
            halves = [flat[row(c, h, r), :] for h in range(2)]
            both = dot(at_ref[...], triple(lanes(*halves)))
            acc_ref[x] = both[0:STATE]
            tr_ref[x] = both[STATE:]

    far = (GX - 1) * (GY - 1)
    def push(turn, carry):
        peer = ((px + 1 + turn // (GY - 1)) % GX, (py + 1 + turn % (GY - 1)) % GY)
        send(peer, GX + GY - 1 + turn)
        return carry

    begin(0)
    pl.semaphore_wait(all_in, GY - 1)
    lax.fori_loop(0, far, push, 0, unroll=7)

    def begin_more(c, carry):
        begin(c)
        return carry

    lax.fori_loop(1, EX // 8, begin_more, 0)
    for part, count in ((0, PART - 1), (1, PART)):
        some = pl.ds(0, count * USED)
        pltpu.make_async_copy(got_ref.at[some], got_ref.at[some], far_sem.at[1 + part]).wait()
        unpack(part, got_ref, pay_ref, col_ref, rowid_ref)
        force(0, (part,), pay_ref, col_ref, rowid_ref, force_ref)

    peers = (
        (lax.rem(px + GX - 1, GX), py),
        (lax.rem(px + 1, GX), py),
        (px, lax.rem(py + GY - 1, GY)),
        (px, lax.rem(py + 1, GY)),
    )

    def send_halos(s, near_ref, down, up):
        ysend[s, 0] = down
        ysend[s, 1] = up
        pairs = (
            (near_ref.at[0, FN : 2 * FN], near_ref.at[EX, FN : 2 * FN]),
            (near_ref.at[EX + 1, 0:FN], near_ref.at[1, 0:FN]),
            (ysend.at[s, 0], yrecv.at[s, 1]),
            (ysend.at[s, 1], yrecv.at[s, 0]),
        )
        copies = []
        for k in range(4):
            copies.append(
                pltpu.make_async_remote_copy(
                    src_ref=pairs[k][0],
                    dst_ref=pairs[k][1],
                    send_sem=near_send.at[s, k],
                    recv_sem=near_recv.at[s, k],
                    device_id=peers[k],
                    device_id_type=MESH,
                )
            )
            copies[-1].start()
        return copies

    def take_halos(s, copies):
        for copy in copies:
            copy.wait()
        rim_ref[0] = jnp.where(py == 0, ysend[s, 0], yrecv[s, 0])
        rim_ref[1] = jnp.where(py == GY - 1, ysend[s, 1], yrecv[s, 1])

    def correct_traces(x, carry):
        tr = dot(c_ref[...], triple(force_ref[0, x]))
        return put(x, tr_ref[x] + tr, near1_ref, carry)

    def middle(x, carry):
        value = finish(
            x, acc_ref, near1_ref, rim_ref, bc_ref, scale_ref, force_ref[0, x]
        )
        hi, lo = split(rows(value[0:NODES] + force_ref[1, x], value[NODES:STATE]))
        slab[x, 0:STATE, :] = hi
        slab[x, STATE : 2 * STATE, :] = lo
        return carry

    def trace(x, carry):
        both = dot(t_ref[...], slab[x, 0:STATE, :])
        tr = dot(t_ref[0 : 4 * FN, :], slab[x, STATE : 2 * STATE, :])
        return put(x, both[0 : 4 * FN] + both[4 * FN : 8 * FN] + tr, near2_ref, carry)

    def hold(x, carry):
        acc_ref[x] = dot(at_ref[0:STATE, :], rows(slab[x], slab[x, 0:STATE, :]))
        return carry

    rim = jnp.zeros((FN, 128), F32)
    down, up = lax.fori_loop(0, EX, correct_traces, (rim, rim), unroll=32)
    copies = send_halos(0, near1_ref, down, up)
    force(1, (0, 1), pay_ref, col_ref, rowid_ref, force_ref)
    take_halos(0, copies)
    lax.fori_loop(0, EX, middle, 0, unroll=32)
    down, up = lax.fori_loop(0, EX, trace, (rim, rim), unroll=32)
    copies = send_halos(1, near2_ref, down, up)
    lax.fori_loop(0, EX, hold, 0, unroll=32)
    take_halos(1, copies)
    rest = pl.ds(0, (DEV - 1) * USED)
    pltpu.make_async_copy(out_ref.at[rest], out_ref.at[rest], far_sem.at[0]).wait()


def last_kernel(acc_ref, near_ref, rim_ref, b_ref, scale_ref, out_ref, stage, sem):
    def store(c, h):
        band = pl.ds(pl.multiple_of(c * 8, 8), 8)
        column = slice(h * 128, h * 128 + 128)
        return pltpu.make_async_copy(
            stage.at[tile(c, h)], out_ref.at[:, band, column], sem.at[c, h]
        )

    flat = stage.reshape(EX // 4 * STATE * 8, 128)

    def body(c, carry):
        for r in range(8):
            value = finish(c * 8 + r, acc_ref, near_ref, rim_ref, b_ref, scale_ref)
            for h in range(2):
                flat[row(c, h, r), :] = value[:, h * 128 : h * 128 + 128]
        for h in range(2):
            store(c, h).start()
        return carry

    lax.fori_loop(0, EX // 8, body, 0)
    for c in range(EX // 8):
        for h in range(2):
            store(c, h).wait()


def local(
    adjoint_state, inverse_scale, element_inverse, trace_op, lift_op,
    obs_elem, obs_count, obs_basis, innovation,
):
    acc, near, rim, lift, scale = pl.pallas_call(
        main_kernel,
        out_shape=(
            pltpu.VMEM((EX, STATE, EY), F32),
            pltpu.VMEM((EX + 2, 4 * FN, EY), F32),
            pltpu.VMEM((2, FN, 128), F32),
            pltpu.VMEM((STATE, 12 * FN), BF),
            pltpu.VMEM((EX, EY), F32),
        ),
        in_specs=[HBM] * 9,
        out_specs=(VMEM,) * 5,
        scratch_shapes=[
            pltpu.VMEM((EX // 4 * STATE, 8, 128), F32),
            pltpu.VMEM((EX, 2 * STATE, EY), BF),
            pltpu.VMEM((EX + 2, 4 * FN, EY), F32),
            pltpu.VMEM((EX, 4 * FN, EY), F32),
            pltpu.VMEM((STEPS, EX, NODES, EY), F32),
            pltpu.VMEM((STEPS, NODES, 2 * OBS), BF),
            pltpu.VMEM((STEPS, 2 * OBS, EY), BF),
            pltpu.VMEM((8, OBS), jnp.int32),
            pltpu.VMEM((STATE + 4 * FN, 3 * STATE), BF),
            pltpu.VMEM((4 * FN, 3 * NODES), BF),
            pltpu.VMEM((STATE, 12 * FN + 3 * NODES), BF),
            pltpu.VMEM((8 * FN, STATE), BF),
            pltpu.VMEM((STATE, STATE), F32),
            pltpu.VMEM((4 * FN, STATE), F32),
            pltpu.VMEM((STATE, 4 * FN), F32),
            pltpu.VMEM((STEPS, OBS), jnp.int32),
            pltpu.VMEM((1, STEPS), jnp.int32),
            pltpu.VMEM((STEPS, NODES, OBS), F32),
            pltpu.VMEM((STEPS, OBS), F32),
            pltpu.VMEM((DEV * 8, 128), F32),
            pltpu.VMEM((DEV * 8, 128), F32),
            pltpu.VMEM((STEPS, 2, FN, 128), F32),
            pltpu.VMEM((STEPS, 2, FN, 128), F32),
            pltpu.SemaphoreType.DMA((EX // 8, 2)),
            pltpu.SemaphoreType.DMA((8,)),
            pltpu.SemaphoreType.DMA((3,)),
            pltpu.SemaphoreType.DMA((STEPS, 4)),
            pltpu.SemaphoreType.DMA((STEPS, 4)),
            pltpu.SemaphoreType.REGULAR,
        ],
        compiler_params=pltpu.CompilerParams(
            collective_id=0, has_side_effects=True, vmem_limit_bytes=40 << 20
        ),
        name="main",
    )(
        *(
            pltpu.with_memory_space_constraint(v, pltpu.HBM)
            for v in (
                adjoint_state, inverse_scale, element_inverse, trace_op, lift_op,
                obs_elem, obs_count.T, obs_basis, innovation,
            )
        )
    )
    return pl.pallas_call(
        last_kernel,
        out_shape=jax.ShapeDtypeStruct((STATE, EX, EY), F32),
        in_specs=[VMEM] * 5,
        out_specs=HBM,
        scratch_shapes=[
            pltpu.VMEM((EX // 4 * STATE, 8, 128), F32),
            pltpu.SemaphoreType.DMA((EX // 8, 2)),
        ],
        compiler_params=pltpu.CompilerParams(vmem_limit_bytes=24 << 20),
        name="last",
    )(acc, near, rim, lift, scale)


def solution(mesh):
    placed = (
        P(None, "gx", "gy"),
        P("gx", "gy"),
        P(),
        P(),
        P(),
        P(None, ("gx", "gy")),
        P(None, ("gx", "gy")),
        P(None, None, ("gx", "gy")),
        P(None, ("gx", "gy")),
    )
    return jax.shard_map(
        local, mesh=mesh, in_specs=placed, out_specs=P(None, "gx", "gy"), check_vma=False
    )
```

```python
import functools

import jax
import jax.numpy as jnp
from jax import lax
from jax.experimental import pallas as pl
from jax.experimental.pallas import tpu as pltpu
from jax.sharding import PartitionSpec as P

F32 = jnp.float32
BF = jnp.bfloat16
MESH = pl.DeviceIdType.MESH
STEPS = 2
NODES = 64
FN = 24
STATE = 192
EX = 32
EY = 256
OBS = 768
CAP = 6
USED = CAP + 1
GX = 8
GY = 16
DEV = GX * GY
PART = DEV // 2
HOT = PART * CAP
VMEM = pl.BlockSpec(memory_space=pltpu.VMEM)
HBM = pl.BlockSpec(memory_space=pltpu.HBM)


def dot(a, b):
    return jnp.dot(a, b, preferred_element_type=F32)


def rows(*parts):
    return jnp.concatenate(parts, axis=0)


def lanes(*parts):
    return jnp.concatenate(parts, axis=1)


def dot_nt(a, b):
    return lax.dot_general(a, b, (((1,), (1,)), ((), ())), preferred_element_type=F32)


def dot_full(a, b):
    return jnp.dot(a, b, preferred_element_type=F32, precision=lax.Precision.HIGHEST)


def split(v):
    hi = v.astype(BF)
    return hi, (v - hi.astype(F32)).astype(BF)


def triple(v):
    hi, lo = split(v)
    return rows(hi, lo, hi)


def weights(*values):
    parts = []
    for v in values:
        hi, lo = split(v)
        hi, lo = hi.astype(F32), lo.astype(F32)
        parts += [hi, hi, lo]
    return lanes(*parts).astype(BF)


def tile(c, h):
    return pl.ds(pl.multiple_of((c * 2 + h) * STATE, 8), STATE)


def row(c, h, r):
    return pl.ds(pl.multiple_of((c * 2 + h) * STATE * 8, 8) + r, STATE, stride=8)


def iota(shape, dim):
    return lax.broadcasted_iota(jnp.int32, shape, dim)


def pack(elem_ref, count_ref, basis_ref, innov_ref, out_ref):
    lane = iota((1, OBS), 1)
    owner = iota((DEV, OBS), 0)
    tri = (iota((256, 256), 0) < iota((256, 256), 1)).astype(F32).astype(BF)
    row = iota((128, OBS), 0)
    halves = []
    ids = jnp.zeros((DEV, 128), F32)
    for s in range(STEPS):
        elem = elem_ref[s : s + 1, :]
        gx = lax.shift_right_logical(elem, 17)
        lx = lax.shift_right_logical(elem, 12) & (EX - 1)
        gy = lax.shift_right_logical(elem, 8) & (GY - 1)
        ly = elem & (EY - 1)
        live = lane < count_ref[0:1, s : s + 1]
        target = jnp.where(live, gx * GY + gy, -1)
        member = (owner == target).astype(F32)
        carry = jnp.zeros((DEV, 1), F32)
        running = []
        for b in range(OBS // 256):
            part = member[:, b * 256 : (b + 1) * 256]
            running.append(dot(part.astype(BF), tri) + carry)
            carry = carry + jnp.sum(part, axis=1, keepdims=True)
        before = jnp.concatenate(running, axis=1)
        rank = jnp.sum(member * before, axis=0, keepdims=True).astype(jnp.int32)
        hi, lo = split(basis_ref[s] * innov_ref[s : s + 1, :])
        both = jnp.concatenate([hi, lo], axis=0)
        picked = []
        for j in range(CAP):
            chosen = jnp.where(rank == j, member, 0.0).astype(BF)
            got = dot_nt(chosen, both)
            picked.append(got + pltpu.roll(got, 64, 1))
        halves.append(picked)
        where = jnp.where(row == rank + 16 * s, lx + 1, 0)
        where = where + jnp.where(row == rank + 16 * s + 8, ly, 0)
        ids = ids + dot_nt(member.astype(BF), where.astype(F32).astype(BF))
    low = iota((DEV, 128), 1) < 64
    for j in range(CAP):
        out_ref[pl.ds(j, DEV, stride=8), :] = jnp.where(low, halves[0][j], halves[1][j])
    out_ref[pl.ds(CAP, DEV, stride=8), :] = ids


def unpack(part, got_ref, pay_ref, col_ref, rowid_ref):
    def get(j):
        return got_ref[pl.ds(part * PART * 8 + j, PART, stride=8), :]

    low = iota((1, 128), 1) < PART
    ids = rows(get(CAP), get(CAP)).T
    values = [rows(get(j), get(j + 1)).T for j in range(0, CAP, 2)]
    for s in range(STEPS):
        hi, lo = split(lanes(*[v[s * NODES : s * NODES + NODES] for v in values]))
        pay_ref[s, :, 2 * HOT * part : 2 * HOT * part + HOT] = hi
        pay_ref[s, :, 2 * HOT * part + HOT : 2 * HOT * (part + 1)] = lo

        def spread(first):
            at = [ids[first + j : first + j + 1, :] for j in range(CAP)]
            at = [jnp.where(low, at[j], at[j + 1]) for j in range(0, CAP, 2)]
            return lanes(*at).astype(jnp.int32)

        rowid_ref[s : s + 1, HOT * part : HOT * part + HOT] = spread(s * 16) - 1
        hot = (iota((EY, HOT), 0) == spread(s * 16 + 8)).astype(F32).T.astype(BF)
        col_ref[s, 2 * HOT * part : 2 * HOT * part + HOT, :] = hot
        col_ref[s, 2 * HOT * part + HOT : 2 * HOT * (part + 1), :] = hot


def force(s, parts, pay_ref, col_ref, rowid_ref, force_ref):
    group = 16
    start, stop = parts[0], parts[-1] + 1

    def body(g, carry):
        rowid = rowid_ref[s : s + 1, HOT * start : HOT * stop]
        pay = pay_ref[s, :, 2 * HOT * start : 2 * HOT * stop]
        stack = []
        for i in range(group):
            here = (rowid == g * group + i).astype(F32).astype(BF)
            here = [here[:, HOT * p : HOT * p + HOT] for p in range(stop - start)]
            stack.append(pay * lanes(*[here[p // 2] for p in range(2 * len(here))]))
        got = dot(rows(*stack), col_ref[s, 2 * HOT * start : 2 * HOT * stop, :])
        for i in range(group):
            mine = got[i * NODES : i * NODES + NODES]
            if start > 0:
                mine = mine + force_ref[s, g * group + i]
            force_ref[s, g * group + i] = mine
        return carry

    lax.fori_loop(0, EX // group, body, 0)


def put(x, tr, near_ref, carry):
    down, up = carry
    near_ref[x, FN : 2 * FN, :] = tr[0:FN]
    near_ref[x + 2, 0:FN, :] = tr[FN : 2 * FN]
    from_south = pltpu.roll(tr[3 * FN : 4 * FN], 1, 1)
    from_north = pltpu.roll(tr[2 * FN : 3 * FN], EY - 1, 1)
    near_ref[x + 1, 2 * FN : 3 * FN, :] = from_south
    near_ref[x + 1, 3 * FN : 4 * FN, :] = from_north
    here = iota((FN, 128), 1) == x
    up = jnp.where(here, from_south[:, 0:1], up)
    down = jnp.where(here, from_north[:, EY - 1 : EY], down)
    return down, up


def finish(x, acc_ref, near_ref, rim_ref, b_ref, scale_ref, force=None):
    lane = iota((FN, 128), 1)
    below = pltpu.roll(rim_ref[0], (128 - x) % 128, 1)
    above = pltpu.roll(rim_ref[1], 127 - x, 1)
    near = near_ref[x + 1]
    south, north = near[2 * FN : 3 * FN], near[3 * FN : 4 * FN]
    south = lanes(jnp.where(lane == 0, below, south[:, 0:128]), south[:, 128:256])
    north = lanes(north[:, 0:128], jnp.where(lane == 127, above, north[:, 128:256]))
    given = triple(rows(near[0 : 2 * FN], south, north))
    if force is not None:
        given = rows(given, triple(force))
    lifted = dot(b_ref[...], given)
    return (acc_ref[x] + lifted) * scale_ref[pl.ds(x, 1), :]


def main_kernel(
    state_hbm, scale_hbm, inverse_hbm, trace_hbm, lift_hbm, elem_hbm, count_hbm, basis_hbm, innov_hbm,
    acc_ref, near2_ref, rim_ref, b_ref, scale_ref,
    stage, slab, near1_ref, tr_ref, force_ref, pay_ref, col_ref, rowid_ref, at_ref, c_ref, bc_ref, t_ref,
    inverse_ref, trace_ref, lift_ref, elem_ref, count_ref, basis_ref, innov_ref,
    out_ref, got_ref, ysend, yrecv,
    load_sem, small_sem, far_sem, near_send, near_recv, all_in,
):
    px, py = lax.axis_index("gx"), lax.axis_index("gy")
    me = px * GY + py
    barrier = pltpu.get_barrier_semaphore()
    row_peers = [((px + k) % GX, py) for k in range(1, GX)]
    column_peers = [(px, (py + k) % GY) for k in range(1, GY)]
    for peer in row_peers + column_peers:
        pl.semaphore_signal(barrier, inc=1, device_id=peer, device_id_type=MESH)
    small = []
    for k, (src, dst) in enumerate(
        (
            (elem_hbm, elem_ref), (count_hbm, count_ref), (basis_hbm, basis_ref),
            (innov_hbm, innov_ref), (inverse_hbm, inverse_ref), (trace_hbm, trace_ref),
            (lift_hbm, lift_ref), (scale_hbm, scale_ref),
        )
    ):
        small.append(pltpu.make_async_copy(src, dst, small_sem.at[k]))
        small[-1].start()

    def load(c, h):
        column = slice(h * 128, h * 128 + 128)
        band = pl.ds(pl.multiple_of(c * 8, 8), 8)
        return pltpu.make_async_copy(
            state_hbm.at[:, band, column], stage.at[tile(c, h)], load_sem.at[c, h]
        )

    for c in range(EX // 8):
        for h in range(2):
            load(c, h).start()
    for copy in small[0:4]:
        copy.wait()
    pack(elem_ref, count_ref, basis_ref, innov_ref, out_ref)
    mine = pl.ds(pl.multiple_of(me * 8, 8), USED)
    got_ref[0:USED, :] = out_ref[mine, :]
    pl.semaphore_wait(barrier, GX + GY - 2)
    for peer in column_peers:
        pl.semaphore_signal(all_in, inc=1, device_id=peer, device_id_type=MESH)

    def send(peer, slot):
        to = peer[0] * GY + peer[1]
        pltpu.make_async_remote_copy(
            src_ref=out_ref.at[pl.ds(pl.multiple_of(to * 8, 8), USED)],
            dst_ref=got_ref.at[pl.ds(pl.multiple_of(slot * 8, 8), USED)],
            send_sem=far_sem.at[0],
            recv_sem=far_sem.at[1 + slot // PART],
            device_id=peer,
            device_id_type=MESH,
        ).start()

    for k, peer in enumerate(row_peers + column_peers):
        send(peer, k + 1)
    for copy in small[4:]:
        copy.wait()
    operator = trace_ref[...]
    inverse = inverse_ref[...]
    half = 0.5 * dot_full(inverse, lift_ref[...])
    whole = inverse + dot_full(half, operator)
    at_ref[...] = weights(rows(whole, operator))
    c_ref[...] = weights(operator[:, 0:NODES])
    bc_ref[...] = weights(half, whole[:, 0:NODES])
    hi, lo = split(operator)
    t_ref[0 : 4 * FN, :] = hi
    t_ref[4 * FN : 8 * FN, :] = lo
    b_ref[...] = weights(half)

    flat = stage.reshape(EX // 4 * STATE * 8, 128)

    def begin(c):
        for h in range(2):
            load(c, h).wait()
        for r in range(8):
            x = c * 8 + r
            halves = [flat[row(c, h, r), :] for h in range(2)]
            both = dot(at_ref[...], triple(lanes(*halves)))
            acc_ref[x] = both[0:STATE]
            tr_ref[x] = both[STATE:]

    far = (GX - 1) * (GY - 1)
    def push(turn, carry):
        peer = ((px + 1 + turn // (GY - 1)) % GX, (py + 1 + turn % (GY - 1)) % GY)
        send(peer, GX + GY - 1 + turn)
        return carry

    begin(0)
    pl.semaphore_wait(all_in, GY - 1)
    lax.fori_loop(0, far, push, 0, unroll=7)

    def begin_more(c, carry):
        begin(c)
        return carry

    lax.fori_loop(1, EX // 8, begin_more, 0)
    for part, count in ((0, PART - 1), (1, PART)):
        some = pl.ds(0, count * USED)
        pltpu.make_async_copy(got_ref.at[some], got_ref.at[some], far_sem.at[1 + part]).wait()
        unpack(part, got_ref, pay_ref, col_ref, rowid_ref)
        force(0, (part,), pay_ref, col_ref, rowid_ref, force_ref)

    peers = (
        (lax.rem(px + GX - 1, GX), py),
        (lax.rem(px + 1, GX), py),
        (px, lax.rem(py + GY - 1, GY)),
        (px, lax.rem(py + 1, GY)),
    )

    def send_halos(s, near_ref, down, up):
        ysend[s, 0] = down
        ysend[s, 1] = up
        pairs = (
            (near_ref.at[0, FN : 2 * FN], near_ref.at[EX, FN : 2 * FN]),
            (near_ref.at[EX + 1, 0:FN], near_ref.at[1, 0:FN]),
            (ysend.at[s, 0], yrecv.at[s, 1]),
            (ysend.at[s, 1], yrecv.at[s, 0]),
        )
        copies = []
        for k in range(4):
            copies.append(
                pltpu.make_async_remote_copy(
                    src_ref=pairs[k][0],
                    dst_ref=pairs[k][1],
                    send_sem=near_send.at[s, k],
                    recv_sem=near_recv.at[s, k],
                    device_id=peers[k],
                    device_id_type=MESH,
                )
            )
            copies[-1].start()
        return copies

    def take_halos(s, copies):
        for copy in copies:
            copy.wait()
        rim_ref[0] = jnp.where(py == 0, ysend[s, 0], yrecv[s, 0])
        rim_ref[1] = jnp.where(py == GY - 1, ysend[s, 1], yrecv[s, 1])

    def correct_traces(x, carry):
        tr = dot(c_ref[...], triple(force_ref[0, x]))
        return put(x, tr_ref[x] + tr, near1_ref, carry)

    def middle(x, carry):
        value = finish(
            x, acc_ref, near1_ref, rim_ref, bc_ref, scale_ref, force_ref[0, x]
        )
        hi, lo = split(rows(value[0:NODES] + force_ref[1, x], value[NODES:STATE]))
        slab[x, 0:STATE, :] = hi
        slab[x, STATE : 2 * STATE, :] = lo
        return carry

    def trace(x, carry):
        both = dot(t_ref[...], slab[x, 0:STATE, :])
        tr = dot(t_ref[0 : 4 * FN, :], slab[x, STATE : 2 * STATE, :])
        return put(x, both[0 : 4 * FN] + both[4 * FN : 8 * FN] + tr, near2_ref, carry)

    def hold(x, carry):
        acc_ref[x] = dot(at_ref[0:STATE, :], rows(slab[x], slab[x, 0:STATE, :]))
        return carry

    rim = jnp.zeros((FN, 128), F32)
    down, up = lax.fori_loop(0, EX, correct_traces, (rim, rim), unroll=32)
    copies = send_halos(0, near1_ref, down, up)
    force(1, (0, 1), pay_ref, col_ref, rowid_ref, force_ref)
    take_halos(0, copies)
    lax.fori_loop(0, EX, middle, 0, unroll=32)
    down, up = lax.fori_loop(0, EX, trace, (rim, rim), unroll=32)
    copies = send_halos(1, near2_ref, down, up)
    lax.fori_loop(0, EX, hold, 0, unroll=32)
    take_halos(1, copies)
    rest = pl.ds(0, (DEV - 1) * USED)
    pltpu.make_async_copy(out_ref.at[rest], out_ref.at[rest], far_sem.at[0]).wait()


def last_kernel(acc_ref, near_ref, rim_ref, b_ref, scale_ref, out_ref, stage, sem):
    def store(c, h):
        band = pl.ds(pl.multiple_of(c * 8, 8), 8)
        column = slice(h * 128, h * 128 + 128)
        return pltpu.make_async_copy(
            stage.at[tile(c, h)], out_ref.at[:, band, column], sem.at[c, h]
        )

    flat = stage.reshape(EX // 4 * STATE * 8, 128)

    def body(c, carry):
        for r in range(8):
            value = finish(c * 8 + r, acc_ref, near_ref, rim_ref, b_ref, scale_ref)
            for h in range(2):
                flat[row(c, h, r), :] = value[:, h * 128 : h * 128 + 128]
        for h in range(2):
            store(c, h).start()
        return carry

    lax.fori_loop(0, EX // 8, body, 0, unroll=True)
    for c in range(EX // 8):
        for h in range(2):
            store(c, h).wait()


def local(
    adjoint_state, inverse_scale, element_inverse, trace_op, lift_op,
    obs_elem, obs_count, obs_basis, innovation,
):
    acc, near, rim, lift, scale = pl.pallas_call(
        main_kernel,
        out_shape=(
            pltpu.VMEM((EX, STATE, EY), F32),
            pltpu.VMEM((EX + 2, 4 * FN, EY), F32),
            pltpu.VMEM((2, FN, 128), F32),
            pltpu.VMEM((STATE, 12 * FN), BF),
            pltpu.VMEM((EX, EY), F32),
        ),
        in_specs=[HBM] * 9,
        out_specs=(VMEM,) * 5,
        scratch_shapes=[
            pltpu.VMEM((EX // 4 * STATE, 8, 128), F32),
            pltpu.VMEM((EX, 2 * STATE, EY), BF),
            pltpu.VMEM((EX + 2, 4 * FN, EY), F32),
            pltpu.VMEM((EX, 4 * FN, EY), F32),
            pltpu.VMEM((STEPS, EX, NODES, EY), F32),
            pltpu.VMEM((STEPS, NODES, 2 * OBS), BF),
            pltpu.VMEM((STEPS, 2 * OBS, EY), BF),
            pltpu.VMEM((8, OBS), jnp.int32),
            pltpu.VMEM((STATE + 4 * FN, 3 * STATE), BF),
            pltpu.VMEM((4 * FN, 3 * NODES), BF),
            pltpu.VMEM((STATE, 12 * FN + 3 * NODES), BF),
            pltpu.VMEM((8 * FN, STATE), BF),
            pltpu.VMEM((STATE, STATE), F32),
            pltpu.VMEM((4 * FN, STATE), F32),
            pltpu.VMEM((STATE, 4 * FN), F32),
            pltpu.VMEM((STEPS, OBS), jnp.int32),
            pltpu.VMEM((1, STEPS), jnp.int32),
            pltpu.VMEM((STEPS, NODES, OBS), F32),
            pltpu.VMEM((STEPS, OBS), F32),
            pltpu.VMEM((DEV * 8, 128), F32),
            pltpu.VMEM((DEV * 8, 128), F32),
            pltpu.VMEM((STEPS, 2, FN, 128), F32),
            pltpu.VMEM((STEPS, 2, FN, 128), F32),
            pltpu.SemaphoreType.DMA((EX // 8, 2)),
            pltpu.SemaphoreType.DMA((8,)),
            pltpu.SemaphoreType.DMA((3,)),
            pltpu.SemaphoreType.DMA((STEPS, 4)),
            pltpu.SemaphoreType.DMA((STEPS, 4)),
            pltpu.SemaphoreType.REGULAR,
        ],
        compiler_params=pltpu.CompilerParams(
            collective_id=0, has_side_effects=True, vmem_limit_bytes=40 << 20
        ),
        name="main",
    )(
        *(
            pltpu.with_memory_space_constraint(v, pltpu.HBM)
            for v in (
                adjoint_state, inverse_scale, element_inverse, trace_op, lift_op,
                obs_elem, obs_count.T, obs_basis, innovation,
            )
        )
    )
    return pl.pallas_call(
        last_kernel,
        out_shape=jax.ShapeDtypeStruct((STATE, EX, EY), F32),
        in_specs=[VMEM] * 5,
        out_specs=HBM,
        scratch_shapes=[
            pltpu.VMEM((EX // 4 * STATE, 8, 128), F32),
            pltpu.SemaphoreType.DMA((EX // 8, 2)),
        ],
        compiler_params=pltpu.CompilerParams(vmem_limit_bytes=24 << 20),
        name="last",
    )(acc, near, rim, lift, scale)


def solution(mesh):
    placed = (
        P(None, "gx", "gy"),
        P("gx", "gy"),
        P(),
        P(),
        P(),
        P(None, ("gx", "gy")),
        P(None, ("gx", "gy")),
        P(None, None, ("gx", "gy")),
        P(None, ("gx", "gy")),
    )
    return jax.shard_map(
        local, mesh=mesh, in_specs=placed, out_specs=P(None, "gx", "gy"), check_vma=False
    )
```

```python
import functools

import jax
import jax.numpy as jnp
from jax import lax
from jax.experimental import pallas as pl
from jax.experimental.pallas import tpu as pltpu
from jax.sharding import PartitionSpec as P

F32 = jnp.float32
BF = jnp.bfloat16
MESH = pl.DeviceIdType.MESH
STEPS = 2
NODES = 64
FN = 24
STATE = 192
EX = 32
EY = 256
OBS = 768
CAP = 6
USED = CAP + 1
GX = 8
GY = 16
DEV = GX * GY
PART = DEV // 2
HOT = PART * CAP
VMEM = pl.BlockSpec(memory_space=pltpu.VMEM)
HBM = pl.BlockSpec(memory_space=pltpu.HBM)


def dot(a, b):
    return jnp.dot(a, b, preferred_element_type=F32)


def rows(*parts):
    return jnp.concatenate(parts, axis=0)


def lanes(*parts):
    return jnp.concatenate(parts, axis=1)


def dot_nt(a, b):
    return lax.dot_general(a, b, (((1,), (1,)), ((), ())), preferred_element_type=F32)


def dot_full(a, b):
    return jnp.dot(a, b, preferred_element_type=F32, precision=lax.Precision.HIGHEST)


def split(v):
    hi = v.astype(BF)
    return hi, (v - hi.astype(F32)).astype(BF)


def triple(v):
    hi, lo = split(v)
    return rows(hi, lo, hi)


def weights(*values):
    parts = []
    for v in values:
        hi, lo = split(v)
        hi, lo = hi.astype(F32), lo.astype(F32)
        parts += [hi, hi, lo]
    return lanes(*parts).astype(BF)


def tile(c, h):
    return pl.ds(pl.multiple_of((c * 2 + h) * STATE, 8), STATE)


def row(c, h, r):
    return pl.ds(pl.multiple_of((c * 2 + h) * STATE * 8, 8) + r, STATE, stride=8)


def iota(shape, dim):
    return lax.broadcasted_iota(jnp.int32, shape, dim)


def pack(elem_ref, count_ref, basis_ref, innov_ref, out_ref):
    lane = iota((1, OBS), 1)
    owner = iota((DEV, OBS), 0)
    tri = (iota((256, 256), 0) < iota((256, 256), 1)).astype(F32).astype(BF)
    row = iota((128, OBS), 0)
    halves = []
    ids = jnp.zeros((DEV, 128), F32)
    for s in range(STEPS):
        elem = elem_ref[s : s + 1, :]
        gx = lax.shift_right_logical(elem, 17)
        lx = lax.shift_right_logical(elem, 12) & (EX - 1)
        gy = lax.shift_right_logical(elem, 8) & (GY - 1)
        ly = elem & (EY - 1)
        live = lane < count_ref[0:1, s : s + 1]
        target = jnp.where(live, gx * GY + gy, -1)
        member = (owner == target).astype(F32)
        carry = jnp.zeros((DEV, 1), F32)
        running = []
        for b in range(OBS // 256):
            part = member[:, b * 256 : (b + 1) * 256]
            running.append(dot(part.astype(BF), tri) + carry)
            carry = carry + jnp.sum(part, axis=1, keepdims=True)
        before = jnp.concatenate(running, axis=1)
        rank = jnp.sum(member * before, axis=0, keepdims=True).astype(jnp.int32)
        hi, lo = split(basis_ref[s] * innov_ref[s : s + 1, :])
        both = jnp.concatenate([hi, lo], axis=0)
        picked = []
        for j in range(CAP):
            chosen = jnp.where(rank == j, member, 0.0).astype(BF)
            got = dot_nt(chosen, both)
            picked.append(got + pltpu.roll(got, 64, 1))
        halves.append(picked)
        where = jnp.where(row == rank + 16 * s, lx + 1, 0)
        where = where + jnp.where(row == rank + 16 * s + 8, ly, 0)
        ids = ids + dot_nt(member.astype(BF), where.astype(F32).astype(BF))
    low = iota((DEV, 128), 1) < 64
    for j in range(CAP):
        out_ref[pl.ds(j, DEV, stride=8), :] = jnp.where(low, halves[0][j], halves[1][j])
    out_ref[pl.ds(CAP, DEV, stride=8), :] = ids


def unpack(part, got_ref, pay_ref, col_ref, rowid_ref):
    def get(j):
        return got_ref[pl.ds(part * PART * 8 + j, PART, stride=8), :]

    low = iota((1, 128), 1) < PART
    ids = rows(get(CAP), get(CAP)).T
    values = [rows(get(j), get(j + 1)).T for j in range(0, CAP, 2)]
    for s in range(STEPS):
        hi, lo = split(lanes(*[v[s * NODES : s * NODES + NODES] for v in values]))
        pay_ref[s, :, 2 * HOT * part : 2 * HOT * part + HOT] = hi
        pay_ref[s, :, 2 * HOT * part + HOT : 2 * HOT * (part + 1)] = lo

        def spread(first):
            at = [ids[first + j : first + j + 1, :] for j in range(CAP)]
            at = [jnp.where(low, at[j], at[j + 1]) for j in range(0, CAP, 2)]
            return lanes(*at).astype(jnp.int32)

        rowid_ref[s : s + 1, HOT * part : HOT * part + HOT] = spread(s * 16) - 1
        hot = (iota((EY, HOT), 0) == spread(s * 16 + 8)).astype(F32).T.astype(BF)
        col_ref[s, 2 * HOT * part : 2 * HOT * part + HOT, :] = hot
        col_ref[s, 2 * HOT * part + HOT : 2 * HOT * (part + 1), :] = hot


def force(s, parts, pay_ref, col_ref, rowid_ref, force_ref):
    group = 16
    start, stop = parts[0], parts[-1] + 1

    def body(g, carry):
        rowid = rowid_ref[s : s + 1, HOT * start : HOT * stop]
        pay = pay_ref[s, :, 2 * HOT * start : 2 * HOT * stop]
        stack = []
        for i in range(group):
            here = (rowid == g * group + i).astype(F32).astype(BF)
            here = [here[:, HOT * p : HOT * p + HOT] for p in range(stop - start)]
            stack.append(pay * lanes(*[here[p // 2] for p in range(2 * len(here))]))
        got = dot(rows(*stack), col_ref[s, 2 * HOT * start : 2 * HOT * stop, :])
        for i in range(group):
            mine = got[i * NODES : i * NODES + NODES]
            if start > 0:
                mine = mine + force_ref[s, g * group + i]
            force_ref[s, g * group + i] = mine
        return carry

    lax.fori_loop(0, EX // group, body, 0, unroll=True)


def put(x, tr, near_ref, carry):
    down, up = carry
    near_ref[x, FN : 2 * FN, :] = tr[0:FN]
    near_ref[x + 2, 0:FN, :] = tr[FN : 2 * FN]
    from_south = pltpu.roll(tr[3 * FN : 4 * FN], 1, 1)
    from_north = pltpu.roll(tr[2 * FN : 3 * FN], EY - 1, 1)
    near_ref[x + 1, 2 * FN : 3 * FN, :] = from_south
    near_ref[x + 1, 3 * FN : 4 * FN, :] = from_north
    here = iota((FN, 128), 1) == x
    up = jnp.where(here, from_south[:, 0:1], up)
    down = jnp.where(here, from_north[:, EY - 1 : EY], down)
    return down, up


def finish(x, acc_ref, near_ref, rim_ref, b_ref, scale_ref, force=None):
    lane = iota((FN, 128), 1)
    below = pltpu.roll(rim_ref[0], (128 - x) % 128, 1)
    above = pltpu.roll(rim_ref[1], 127 - x, 1)
    near = near_ref[x + 1]
    south, north = near[2 * FN : 3 * FN], near[3 * FN : 4 * FN]
    south = lanes(jnp.where(lane == 0, below, south[:, 0:128]), south[:, 128:256])
    north = lanes(north[:, 0:128], jnp.where(lane == 127, above, north[:, 128:256]))
    given = triple(rows(near[0 : 2 * FN], south, north))
    if force is not None:
        given = rows(given, triple(force))
    lifted = dot(b_ref[...], given)
    return (acc_ref[x] + lifted) * scale_ref[pl.ds(x, 1), :]


def main_kernel(
    state_hbm, scale_hbm, inverse_hbm, trace_hbm, lift_hbm, elem_hbm, count_hbm, basis_hbm, innov_hbm,
    acc_ref, near2_ref, rim_ref, b_ref, scale_ref,
    stage, slab, near1_ref, tr_ref, force_ref, pay_ref, col_ref, rowid_ref, at_ref, c_ref, bc_ref, t_ref,
    inverse_ref, trace_ref, lift_ref, elem_ref, count_ref, basis_ref, innov_ref,
    out_ref, got_ref, ysend, yrecv,
    load_sem, small_sem, far_sem, near_send, near_recv, all_in,
):
    px, py = lax.axis_index("gx"), lax.axis_index("gy")
    me = px * GY + py
    barrier = pltpu.get_barrier_semaphore()
    row_peers = [((px + k) % GX, py) for k in range(1, GX)]
    column_peers = [(px, (py + k) % GY) for k in range(1, GY)]
    for peer in row_peers + column_peers:
        pl.semaphore_signal(barrier, inc=1, device_id=peer, device_id_type=MESH)
    small = []
    for k, (src, dst) in enumerate(
        (
            (elem_hbm, elem_ref), (count_hbm, count_ref), (basis_hbm, basis_ref),
            (innov_hbm, innov_ref), (inverse_hbm, inverse_ref), (trace_hbm, trace_ref),
            (lift_hbm, lift_ref), (scale_hbm, scale_ref),
        )
    ):
        small.append(pltpu.make_async_copy(src, dst, small_sem.at[k]))
        small[-1].start()

    def load(c, h):
        column = slice(h * 128, h * 128 + 128)
        band = pl.ds(pl.multiple_of(c * 8, 8), 8)
        return pltpu.make_async_copy(
            state_hbm.at[:, band, column], stage.at[tile(c, h)], load_sem.at[c, h]
        )

    for c in range(EX // 8):
        for h in range(2):
            load(c, h).start()
    for copy in small[0:4]:
        copy.wait()
    pack(elem_ref, count_ref, basis_ref, innov_ref, out_ref)
    mine = pl.ds(pl.multiple_of(me * 8, 8), USED)
    got_ref[0:USED, :] = out_ref[mine, :]
    pl.semaphore_wait(barrier, GX + GY - 2)
    for peer in column_peers:
        pl.semaphore_signal(all_in, inc=1, device_id=peer, device_id_type=MESH)

    def send(peer, slot):
        to = peer[0] * GY + peer[1]
        pltpu.make_async_remote_copy(
            src_ref=out_ref.at[pl.ds(pl.multiple_of(to * 8, 8), USED)],
            dst_ref=got_ref.at[pl.ds(pl.multiple_of(slot * 8, 8), USED)],
            send_sem=far_sem.at[0],
            recv_sem=far_sem.at[1 + slot // PART],
            device_id=peer,
            device_id_type=MESH,
        ).start()

    for k, peer in enumerate(row_peers + column_peers):
        send(peer, k + 1)
    for copy in small[4:]:
        copy.wait()
    operator = trace_ref[...]
    inverse = inverse_ref[...]
    half = 0.5 * dot_full(inverse, lift_ref[...])
    whole = inverse + dot_full(half, operator)
    at_ref[...] = weights(rows(whole, operator))
    c_ref[...] = weights(operator[:, 0:NODES])
    bc_ref[...] = weights(half, whole[:, 0:NODES])
    hi, lo = split(operator)
    t_ref[0 : 4 * FN, :] = hi
    t_ref[4 * FN : 8 * FN, :] = lo
    b_ref[...] = weights(half)

    flat = stage.reshape(EX // 4 * STATE * 8, 128)

    def begin(c):
        for h in range(2):
            load(c, h).wait()
        for r in range(8):
            x = c * 8 + r
            halves = [flat[row(c, h, r), :] for h in range(2)]
            both = dot(at_ref[...], triple(lanes(*halves)))
            acc_ref[x] = both[0:STATE]
            tr_ref[x] = both[STATE:]

    far = (GX - 1) * (GY - 1)
    def push(turn, carry):
        peer = ((px + 1 + turn // (GY - 1)) % GX, (py + 1 + turn % (GY - 1)) % GY)
        send(peer, GX + GY - 1 + turn)
        return carry

    begin(0)
    pl.semaphore_wait(all_in, GY - 1)
    lax.fori_loop(0, far, push, 0, unroll=7)

    def begin_more(c, carry):
        begin(c)
        return carry

    lax.fori_loop(1, EX // 8, begin_more, 0, unroll=True)
    for part, count in ((0, PART - 1), (1, PART)):
        some = pl.ds(0, count * USED)
        pltpu.make_async_copy(got_ref.at[some], got_ref.at[some], far_sem.at[1 + part]).wait()
        unpack(part, got_ref, pay_ref, col_ref, rowid_ref)
        force(0, (part,), pay_ref, col_ref, rowid_ref, force_ref)

    peers = (
        (lax.rem(px + GX - 1, GX), py),
        (lax.rem(px + 1, GX), py),
        (px, lax.rem(py + GY - 1, GY)),
        (px, lax.rem(py + 1, GY)),
    )

    def send_halos(s, near_ref, down, up):
        ysend[s, 0] = down
        ysend[s, 1] = up
        pairs = (
            (near_ref.at[0, FN : 2 * FN], near_ref.at[EX, FN : 2 * FN]),
            (near_ref.at[EX + 1, 0:FN], near_ref.at[1, 0:FN]),
            (ysend.at[s, 0], yrecv.at[s, 1]),
            (ysend.at[s, 1], yrecv.at[s, 0]),
        )
        copies = []
        for k in range(4):
            copies.append(
                pltpu.make_async_remote_copy(
                    src_ref=pairs[k][0],
                    dst_ref=pairs[k][1],
                    send_sem=near_send.at[s, k],
                    recv_sem=near_recv.at[s, k],
                    device_id=peers[k],
                    device_id_type=MESH,
                )
            )
            copies[-1].start()
        return copies

    def take_halos(s, copies):
        for copy in copies:
            copy.wait()
        rim_ref[0] = jnp.where(py == 0, ysend[s, 0], yrecv[s, 0])
        rim_ref[1] = jnp.where(py == GY - 1, ysend[s, 1], yrecv[s, 1])

    def correct_traces(x, carry):
        tr = dot(c_ref[...], triple(force_ref[0, x]))
        return put(x, tr_ref[x] + tr, near1_ref, carry)

    def middle(x, carry):
        value = finish(
            x, acc_ref, near1_ref, rim_ref, bc_ref, scale_ref, force_ref[0, x]
        )
        hi, lo = split(rows(value[0:NODES] + force_ref[1, x], value[NODES:STATE]))
        slab[x, 0:STATE, :] = hi
        slab[x, STATE : 2 * STATE, :] = lo
        return carry

    def trace(x, carry):
        both = dot(t_ref[...], slab[x, 0:STATE, :])
        tr = dot(t_ref[0 : 4 * FN, :], slab[x, STATE : 2 * STATE, :])
        return put(x, both[0 : 4 * FN] + both[4 * FN : 8 * FN] + tr, near2_ref, carry)

    def hold(x, carry):
        acc_ref[x] = dot(at_ref[0:STATE, :], rows(slab[x], slab[x, 0:STATE, :]))
        return carry

    rim = jnp.zeros((FN, 128), F32)
    down, up = lax.fori_loop(0, EX, correct_traces, (rim, rim), unroll=32)
    copies = send_halos(0, near1_ref, down, up)
    force(1, (0, 1), pay_ref, col_ref, rowid_ref, force_ref)
    take_halos(0, copies)
    lax.fori_loop(0, EX, middle, 0, unroll=32)
    down, up = lax.fori_loop(0, EX, trace, (rim, rim), unroll=32)
    copies = send_halos(1, near2_ref, down, up)
    lax.fori_loop(0, EX, hold, 0, unroll=32)
    take_halos(1, copies)
    rest = pl.ds(0, (DEV - 1) * USED)
    pltpu.make_async_copy(out_ref.at[rest], out_ref.at[rest], far_sem.at[0]).wait()


def last_kernel(acc_ref, near_ref, rim_ref, b_ref, scale_ref, out_ref, stage, sem):
    def store(c, h):
        band = pl.ds(pl.multiple_of(c * 8, 8), 8)
        column = slice(h * 128, h * 128 + 128)
        return pltpu.make_async_copy(
            stage.at[tile(c, h)], out_ref.at[:, band, column], sem.at[c, h]
        )

    flat = stage.reshape(EX // 4 * STATE * 8, 128)

    def body(c, carry):
        for r in range(8):
            value = finish(c * 8 + r, acc_ref, near_ref, rim_ref, b_ref, scale_ref)
            for h in range(2):
                flat[row(c, h, r), :] = value[:, h * 128 : h * 128 + 128]
        for h in range(2):
            store(c, h).start()
        return carry

    lax.fori_loop(0, EX // 8, body, 0, unroll=True)
    for c in range(EX // 8):
        for h in range(2):
            store(c, h).wait()


def local(
    adjoint_state, inverse_scale, element_inverse, trace_op, lift_op,
    obs_elem, obs_count, obs_basis, innovation,
):
    acc, near, rim, lift, scale = pl.pallas_call(
        main_kernel,
        out_shape=(
            pltpu.VMEM((EX, STATE, EY), F32),
            pltpu.VMEM((EX + 2, 4 * FN, EY), F32),
            pltpu.VMEM((2, FN, 128), F32),
            pltpu.VMEM((STATE, 12 * FN), BF),
            pltpu.VMEM((EX, EY), F32),
        ),
        in_specs=[HBM] * 9,
        out_specs=(VMEM,) * 5,
        scratch_shapes=[
            pltpu.VMEM((EX // 4 * STATE, 8, 128), F32),
            pltpu.VMEM((EX, 2 * STATE, EY), BF),
            pltpu.VMEM((EX + 2, 4 * FN, EY), F32),
            pltpu.VMEM((EX, 4 * FN, EY), F32),
            pltpu.VMEM((STEPS, EX, NODES, EY), F32),
            pltpu.VMEM((STEPS, NODES, 2 * OBS), BF),
            pltpu.VMEM((STEPS, 2 * OBS, EY), BF),
            pltpu.VMEM((8, OBS), jnp.int32),
            pltpu.VMEM((STATE + 4 * FN, 3 * STATE), BF),
            pltpu.VMEM((4 * FN, 3 * NODES), BF),
            pltpu.VMEM((STATE, 12 * FN + 3 * NODES), BF),
            pltpu.VMEM((8 * FN, STATE), BF),
            pltpu.VMEM((STATE, STATE), F32),
            pltpu.VMEM((4 * FN, STATE), F32),
            pltpu.VMEM((STATE, 4 * FN), F32),
            pltpu.VMEM((STEPS, OBS), jnp.int32),
            pltpu.VMEM((1, STEPS), jnp.int32),
            pltpu.VMEM((STEPS, NODES, OBS), F32),
            pltpu.VMEM((STEPS, OBS), F32),
            pltpu.VMEM((DEV * 8, 128), F32),
            pltpu.VMEM((DEV * 8, 128), F32),
            pltpu.VMEM((STEPS, 2, FN, 128), F32),
            pltpu.VMEM((STEPS, 2, FN, 128), F32),
            pltpu.SemaphoreType.DMA((EX // 8, 2)),
            pltpu.SemaphoreType.DMA((8,)),
            pltpu.SemaphoreType.DMA((3,)),
            pltpu.SemaphoreType.DMA((STEPS, 4)),
            pltpu.SemaphoreType.DMA((STEPS, 4)),
            pltpu.SemaphoreType.REGULAR,
        ],
        compiler_params=pltpu.CompilerParams(
            collective_id=0, has_side_effects=True, vmem_limit_bytes=40 << 20
        ),
        name="main",
    )(
        *(
            pltpu.with_memory_space_constraint(v, pltpu.HBM)
            for v in (
                adjoint_state, inverse_scale, element_inverse, trace_op, lift_op,
                obs_elem, obs_count.T, obs_basis, innovation,
            )
        )
    )
    return pl.pallas_call(
        last_kernel,
        out_shape=jax.ShapeDtypeStruct((STATE, EX, EY), F32),
        in_specs=[VMEM] * 5,
        out_specs=HBM,
        scratch_shapes=[
            pltpu.VMEM((EX // 4 * STATE, 8, 128), F32),
            pltpu.SemaphoreType.DMA((EX // 8, 2)),
        ],
        compiler_params=pltpu.CompilerParams(vmem_limit_bytes=24 << 20),
        name="last",
    )(acc, near, rim, lift, scale)


def solution(mesh):
    placed = (
        P(None, "gx", "gy"),
        P("gx", "gy"),
        P(),
        P(),
        P(),
        P(None, ("gx", "gy")),
        P(None, ("gx", "gy")),
        P(None, None, ("gx", "gy")),
        P(None, ("gx", "gy")),
    )
    return jax.shard_map(
        local, mesh=mesh, in_specs=placed, out_specs=P(None, "gx", "gy"), check_vma=False
    )
```
